256 devices in a mesh: band: 8 (over x_lo, y), dom: 32 (over x_hi, z, core).
Axes of the slice: x: 4 (x_hi: 2, x_lo: 2; x = x_hi * 2 + x_lo), y: 4, z: 8, core: 2. Of those that a mesh axis runs over, the one named last changes fastest.
Arguments:
- partial_density: float32 [8, 192, 96, 128], P('band', 'dom'), may hold values from 0.002 to 0.1
- moments: bfloat16 [9, 256], P(None, 'dom'), may hold values from 0.0099487305 to 0.099609375
- shape_functions: bfloat16 [256, 9, 6912], P('dom'), may hold values from 0.099609375 to 1
- sphere_offsets: int32 [3, 256], P(None, 'dom'), may hold values from 0 to 232, as said below
- owned_count: int32 [32], P('dom'), may hold values from 1 to 8, as said below
Outputs:
- potential: float32 [192, 96, 128], P('dom')
The draws below stay inside these ranges and needn't reach their ends.
Inputs may be any that keep to these rules, and one draw needn't show every extreme that they name: `sphere_offsets`: row 0 lies in 0 to 11, and in 0 to 0 for the last slab; row 1 in 0 to 168; row 2 in 0 to 232; each upper end is reached. `owned_count`: some slab owns exactly 8 atoms.
All inputs are finite; a program needn't handle non-finite values.
Results may differ from the reference program's by a relative error of at most 0.0003.
Values sent between devices are 32-bit elements; how exact they have to be, the bound alone decides.
No kernel may reach another device: no remote copies, remote signals or barrier semaphores. Data moves between devices by JAX's collectives and lax.ppermute only.
A program may use at most 64 MiB of HBM per device.

```python
import math
import jax
import jax.numpy as jnp
from jax import lax

CX = 6
CY = 96
CZ = 128
SLOTS = 8
NL = 9
SBX = 12
SBY = 24
SBZ = 24
BLOCK = 6912
GROUPS = 8
NX = 192
SLOTS_ALL = 256
N_DOM = 32


def draw_owned_count(key, part):
    key = jax.random.fold_in(key, 11)
    first_key, second_key = jax.random.split(key)
    raw_counts = jax.random.randint(first_key, (N_DOM,), 0, SLOTS)
    counts = 1 + raw_counts * raw_counts // SLOTS
    chosen = jax.random.randint(second_key, (), 0, N_DOM)
    return jnp.where(jnp.arange(N_DOM) == chosen, SLOTS, counts).astype(jnp.int32)


def draw_sphere_offsets(key, part):
    key = jax.random.fold_in(key, 23)
    first_key, second_key, third_key = jax.random.split(key, 3)
    slot_total = SLOTS * N_DOM
    brick = jnp.arange(slot_total) // SLOTS
    upper_row = jnp.where(brick == N_DOM - 1, 2 * CX - SBX + 1, 2 * CX)
    row_offset = jax.random.randint(first_key, (slot_total,), 0, upper_row)
    row_offset = row_offset.at[0].set(jnp.where(N_DOM == 1, 2 * CX - SBX, 2 * CX - 1))
    col_offset = jax.random.randint(second_key, (slot_total,), 0, 2 * CY - SBY + 1)
    col_offset = col_offset.at[0].set(2 * CY - SBY)
    depth_offset = jax.random.randint(third_key, (slot_total,), 0, 2 * CZ - SBZ + 1)
    depth_offset = depth_offset.at[0].set(2 * CZ - SBZ).at[1].set(0)
    return jnp.stack([row_offset, col_offset, depth_offset]).astype(jnp.int32)


def block_scale(own_key, extent, shards, low, high):
    def one(axis_at, blocks):
        steps = jax.random.uniform(jax.random.fold_in(jax.random.fold_in(own_key, 6), axis_at), (blocks,), jnp.float32, low / len(shards), high / len(shards))
        return jnp.repeat(jnp.exp(steps), extent[axis_at] // blocks).reshape((-1,) + (1,) * (len(extent) - axis_at - 1))

    level = one(*shards[0])
    for cut in shards[1:]:
        level = level * one(*cut)
    return level


def setup_inputs(seed: int = 0) -> dict:
    key_of = jax.random.split(jax.random.key(seed), 6)
    return {
        "partial_density": jnp.clip(jnp.exp(math.log(0.1) - 3.912023 * jax.random.uniform(key_of[0], (GROUPS, NX, CY, CZ), jnp.float32) ** block_scale(key_of[0], (GROUPS, NX, CY, CZ), ((0, 8), (1, 32)), -0.2, 0.2)), 0.002, 0.1),
        "moments": jnp.clip(jnp.exp(math.log(0.099609375) - 2.3038113 * jax.random.uniform(key_of[1], (NL, SLOTS_ALL), jnp.float32) ** block_scale(key_of[1], (NL, SLOTS_ALL), ((1, 32),), -0.2, 0.2)), 0.0099487305, 0.099609375).astype(jnp.bfloat16),
        "shape_functions": jnp.clip(jnp.exp(math.log(1.0) - 2.306499 * jax.random.uniform(key_of[2], (SLOTS_ALL, NL, BLOCK), jnp.float32) ** block_scale(key_of[2], (SLOTS_ALL, NL, BLOCK), ((0, 32),), -0.2, 0.2)), 0.099609375, 1.0).astype(jnp.bfloat16),
        "sphere_offsets": draw_sphere_offsets(jax.random.fold_in(key_of[5], 71), 0),
        "owned_count": draw_owned_count(jax.random.fold_in(key_of[5], 71), 0),
    }


kappa_pbe = 0.804
mu_pbe = 0.2195
exchange_prefactor = -0.75 * (3.0 / 3.141592653589793) ** (1.0 / 3.0)
gradient_scale = 4.0 * (3.0 * 3.141592653589793 ** 2) ** (2.0 / 3.0)
half_inverse = 0.5 / 0.2


def refine(extended, direction):
    length = extended.shape[direction] - 2
    lower_cells = lax.slice_in_dim(extended, 0, length, axis=direction)
    middle_cells = lax.slice_in_dim(extended, 1, length + 1, axis=direction)
    upper_cells = lax.slice_in_dim(extended, 2, length + 2, axis=direction)
    even_cells = 0.75 * middle_cells + 0.25 * lower_cells
    odd_cells = 0.75 * middle_cells + 0.25 * upper_cells
    joined = jnp.stack([even_cells, odd_cells], axis=direction + 1)
    target = list(middle_cells.shape)
    target[direction] = 2 * length
    return joined.reshape(target)


def restrict(extended, direction):
    doubled = extended.shape[direction] - 2
    halved = doubled // 2

    def paired(start):
        piece = lax.slice_in_dim(extended, start, start + doubled, axis=direction)
        target = list(piece.shape)
        target[direction:direction + 1] = [halved, 2]
        return piece.reshape(target)

    centre = paired(1)
    outer_low = lax.index_in_dim(paired(0), 0, direction + 1, keepdims=False)
    outer_high = lax.index_in_dim(paired(2), 1, direction + 1, keepdims=False)
    first_half = lax.index_in_dim(centre, 0, direction + 1, keepdims=False)
    second_half = lax.index_in_dim(centre, 1, direction + 1, keepdims=False)
    return 0.125 * outer_low + 0.375 * (first_half + second_half) + 0.125 * outer_high


def exchange_parts(density, sigma):
    cube_root = jnp.cbrt(density)
    four_thirds = density * cube_root
    reduced = sigma / (gradient_scale * four_thirds * four_thirds)
    damped = 1.0 + mu_pbe * reduced / kappa_pbe
    enhance = 1.0 + kappa_pbe - kappa_pbe / damped
    slope = mu_pbe / (damped * damped)
    by_density = exchange_prefactor * cube_root * ((4.0 / 3.0) * enhance - (8.0 / 3.0) * reduced * slope)
    by_sigma = exchange_prefactor * slope / (gradient_scale * four_thirds)
    return by_density, by_sigma


def gradients(extended):
    grad_x = (extended[2:, 1:-1, 1:-1] - extended[:-2, 1:-1, 1:-1]) * half_inverse
    grad_y = (extended[1:-1, 2:, 1:-1] - extended[1:-1, :-2, 1:-1]) * half_inverse
    grad_z = (extended[1:-1, 1:-1, 2:] - extended[1:-1, 1:-1, :-2]) * half_inverse
    return grad_x, grad_y, grad_z


def divergence(extended):
    total = extended[0, 2:, 1:-1, 1:-1] - extended[0, :-2, 1:-1, 1:-1]
    total = total + extended[1, 1:-1, 2:, 1:-1] - extended[1, 1:-1, :-2, 1:-1]
    total = total + extended[2, 1:-1, 1:-1, 2:] - extended[2, 1:-1, 1:-1, :-2]
    return total * half_inverse


def reference(partial_density, moments, shape_functions, sphere_offsets, owned_count):
    coarse = jnp.sum(partial_density, axis=0)
    fine = jnp.pad(coarse, 1)
    for direction in range(3):
        fine = refine(fine, direction)
    fine_x, fine_y, fine_z = fine.shape
    slab_rows = 2 * CX
    slot_total = moments.shape[1]
    slot_index = jnp.arange(slot_total).astype(jnp.int32)
    owner = slot_index // SLOTS
    live = ((slot_index % SLOTS) < owned_count[owner]).astype(jnp.float32)
    weights = moments.astype(jnp.float32) * live[None, :]
    blocks = jnp.einsum("ls,slk->sk", weights, shape_functions.astype(jnp.float32))
    position = jnp.arange(BLOCK).astype(jnp.int32)
    along_x = position // (SBY * SBZ)
    along_y = (position // SBZ) % SBY
    along_z = position % SBZ
    rows = (owner * slab_rows + sphere_offsets[0])[:, None] + along_x[None, :]
    cols = sphere_offsets[1][:, None] + along_y[None, :]
    depth = sphere_offsets[2][:, None] + along_z[None, :]
    flat_index = (rows * fine_y + cols) * fine_z + depth
    spheres = jnp.zeros((fine_x * fine_y * fine_z,), jnp.float32).at[flat_index.reshape(-1)].add(blocks.reshape(-1))
    density = fine + spheres.reshape(fine_x, fine_y, fine_z)
    grad_x, grad_y, grad_z = gradients(jnp.pad(density, 1))
    sigma = grad_x * grad_x + grad_y * grad_y + grad_z * grad_z
    by_density, by_sigma = exchange_parts(density, sigma)
    flux = jnp.stack([2.0 * by_sigma * grad_x, 2.0 * by_sigma * grad_y, 2.0 * by_sigma * grad_z])
    fine_potential = by_density - divergence(jnp.pad(flux, ((0, 0), (1, 1), (1, 1), (1, 1))))
    potential = jnp.pad(fine_potential, 1)
    for direction in range(3):
        potential = restrict(potential, direction)
    return potential
```

```python
import functools

import jax
import jax.numpy as jnp
from jax import lax
from jax.experimental import pallas as pl
from jax.experimental.pallas import tpu as pltpu
from jax.sharding import PartitionSpec as P

SLOTS = 8
SBX = 12
SBY = 24
SBZ = 24
CX = 6
FX = 12
RIM = 2
PARTS = 8
YB = 12
WY = 16
CZ = 128
FAR = -4096

KAPPA = 0.804
MU = 0.2195
PREFACTOR = -0.75 * (3.0 / 3.141592653589793) ** (1.0 / 3.0)
SCALE = 4.0 * (3.0 * 3.141592653589793**2) ** (2.0 / 3.0)
HALF_INVERSE = 0.5 / 0.2
DAMP = MU / KAPPA * HALF_INVERSE**2 / SCALE
B0 = PREFACTOR * 4.0 / 3.0 * (1.0 + KAPPA)
B1 = PREFACTOR * -4.0 * KAPPA
B2 = PREFACTOR * 8.0 / 3.0 * KAPPA
FLUX = 2.0 * HALF_INVERSE**2 * PREFACTOR * MU / SCALE


def place_kernel(meta, blocks, out, send_core, send_chip, total):
    for odd_z in range(2):
        total[odd_z, pl.ds(12, 12), pl.ds(24, 32), :] = jnp.zeros((12, 32, 128), jnp.float32)
    column = lax.broadcasted_iota(jnp.int32, (128, 256), 1)
    fine_z = jnp.where(column < 128, 2 * column, 2 * column - 255)
    inner_z = fine_z - lax.broadcasted_iota(jnp.int32, (128, 256), 0)
    row_z = lax.broadcasted_iota(jnp.int32, (128, 256), 0) < SBZ
    first_row = meta[48]
    for source in range(2):

        def one(slot, carry):
            row = meta[source * 24 + slot]
            col = meta[source * 24 + 8 + slot] - first_row + 24
            depth = meta[source * 24 + 16 + slot]

            @pl.when((col > 0) & (col < 56))
            def _():
                shift = lax.rem(col, 8)
                base = pl.multiple_of(col - shift, 8)
                block = blocks[source * SLOTS + slot]
                block = pltpu.roll(block, shift, 1).reshape(SBX * 32, 128)
                high = block.astype(jnp.bfloat16)
                low = (block - high.astype(jnp.float32)).astype(jnp.bfloat16)
                pick = jnp.where((inner_z == depth) & row_z, 1.0, 0.0).astype(jnp.bfloat16)
                spread = jnp.dot(high, pick, preferred_element_type=jnp.float32)
                spread = spread + jnp.dot(low, pick, preferred_element_type=jnp.float32)
                planes = pl.ds(row + 12 * (1 - source), SBX)
                rows = pl.ds(base, 32)
                spread = spread.reshape(SBX, 32, 256)
                for odd_z in range(2):
                    half = spread[:, :, 128 * odd_z : 128 * odd_z + 128]
                    total[odd_z, planes, rows, :] = total[odd_z, planes, rows, :] + half

            return carry

        lax.fori_loop(0, SLOTS, one, 0)
    for plane in range(12):
        for odd_y in range(2):
            for odd_z in range(2):
                rows = pl.ds(24 + odd_y, WY, stride=2)
                out[plane, odd_y, odd_z] = total[odd_z, plane + 12, rows, :]
    upper = meta[49] == 0

    @pl.when(upper)
    def _():
        send_core[...] = out[9:12]
        send_chip[...] = out[0:3]

    @pl.when(jnp.logical_not(upper))
    def _():
        send_core[...] = out[0:3]
        send_chip[...] = out[9:12]


def main_kernel(place, own, core, chip, dots, dots_core, dots_chip, out, dens, flux_x, value):
    slab = place[0]
    part = place[1]
    last = place[2]
    even_slab = lax.rem(slab, 2) == 0
    lane = lax.broadcasted_iota(jnp.int32, (WY, CZ), 1)
    first_lane = lane == 0
    last_lane = lane == CZ - 1
    row = lax.broadcasted_iota(jnp.int32, (WY, CZ), 0) + (YB * part - RIM)
    inside = (row >= 0) & (row < PARTS * YB)

    def row_before(x):
        return pltpu.roll(x, 1, 0)

    def row_after(x):
        return pltpu.roll(x, WY - 1, 0)

    def lane_before(x):
        return jnp.where(first_lane, 0.0, pltpu.roll(x, 1, 1))

    def lane_after(x):
        return jnp.where(last_lane, 0.0, pltpu.roll(x, CZ - 1, 1))

    def coarse(index):
        if index < 0:
            return jnp.where(even_slab, chip[index + 2], core[index + 2])
        if index >= CX:
            return jnp.where(even_slab, core[index - CX], chip[index - CX])
        return own[index]

    def spread(cells):
        middle = 0.75 * cells
        rows = [middle + 0.25 * row_before(cells), middle + 0.25 * row_after(cells)]
        result = []
        for cells_y in rows:
            middle = 0.75 * cells_y
            result.append(
                [middle + 0.25 * lane_before(cells_y), middle + 0.25 * lane_after(cells_y)]
            )
        return result

    def sphere(plane, odd_y, odd_z):
        if plane < 0:
            return jnp.where(
                even_slab, dots_chip[plane + 3, odd_y, odd_z], dots_core[plane + 3, odd_y, odd_z]
            )
        if plane >= FX:
            return jnp.where(
                even_slab, dots_core[plane - FX, odd_y, odd_z], dots_chip[plane - FX, odd_y, odd_z]
            )
        return dots[plane, odd_y, odd_z]

    def in_grid(plane):
        if plane < 0:
            return slab > 0
        if plane >= FX:
            return slab < last
        return None

    grids = {}
    for plane in range(-3, FX + 3):
        index, odd = plane // 2, plane % 2
        near = index + (1 if odd else -1)
        for which in (index, near):
            if which not in grids:
                grids[which] = spread(coarse(which))
        for old in [k for k in grids if k < min(index, near) - 1]:
            del grids[old]
        there = in_grid(plane)
        ok = inside if there is None else inside & there
        for odd_y in range(2):
            for odd_z in range(2):
                cells = 0.75 * grids[index][odd_y][odd_z] + 0.25 * grids[near][odd_y][odd_z]
                cells = cells + sphere(plane, odd_y, odd_z)
                dens[plane + 3, odd_y, odd_z] = jnp.where(ok, cells, 0.0)

    def density(plane):
        return [[dens[plane + 3, odd_y, odd_z] for odd_z in range(2)] for odd_y in range(2)]

    def differences(field_y, field_z):
        along_y = [[None] * 2 for _ in range(2)]
        along_z = [[None] * 2 for _ in range(2)]
        for other in range(2):
            along_y[0][other] = field_y[1][other] - row_before(field_y[1][other])
            along_y[1][other] = row_after(field_y[0][other]) - field_y[0][other]
            along_z[other][0] = field_z[other][1] - lane_before(field_z[other][1])
            along_z[other][1] = lane_after(field_z[other][0]) - field_z[other][0]
        return along_y, along_z

    def store_flux(plane):
        there = in_grid(plane)
        ok = inside if there is None else inside & there
        here = density(plane)
        grad_y, grad_z = differences(here, here)
        flux_y = [[None] * 2 for _ in range(2)]
        flux_z = [[None] * 2 for _ in range(2)]
        by_density = [[None] * 2 for _ in range(2)]
        for odd_y in range(2):
            for odd_z in range(2):
                grad_x = dens[plane + 4, odd_y, odd_z] - dens[plane + 2, odd_y, odd_z]
                gy, gz = grad_y[odd_y][odd_z], grad_z[odd_y][odd_z]
                squared = grad_x * grad_x + gy * gy + gz * gz
                cells = jnp.where(ok, here[odd_y][odd_z], 1.0)
                inverse_root = jnp.exp(jnp.log(cells) * (-1.0 / 3.0))
                power_2 = inverse_root * inverse_root
                power_4 = power_2 * power_2
                inverse = 1.0 / (1.0 + DAMP * squared * (power_4 * power_4))
                by_density[odd_y][odd_z] = cells * power_2 * (B0 + inverse * (B1 + B2 * inverse))
                weight = jnp.where(ok, FLUX * power_4 * (inverse * inverse), 0.0)
                flux_x[plane + 2, odd_y, odd_z] = weight * grad_x
                flux_y[odd_y][odd_z] = weight * gy
                flux_z[odd_y][odd_z] = weight * gz
        if -1 <= plane <= FX:
            spread_y, spread_z = differences(flux_y, flux_z)
            for odd_y in range(2):
                for odd_z in range(2):
                    value[plane + 1, odd_y, odd_z] = by_density[odd_y][odd_z] - (
                        spread_y[odd_y][odd_z] + spread_z[odd_y][odd_z]
                    )

    for plane in range(-2, FX + 2):
        store_flux(plane)

    def potential(plane, odd_y, odd_z):
        there = in_grid(plane)
        ok = inside if there is None else inside & there
        cells = value[plane + 1, odd_y, odd_z] - (
            flux_x[plane + 3, odd_y, odd_z] - flux_x[plane + 1, odd_y, odd_z]
        )
        return jnp.where(ok, cells, 0.0)

    for index in range(CX):
        depth = [None, None]
        for odd_z in range(2):
            rows = []
            for odd_y in range(2):
                low = potential(2 * index - 1, odd_y, odd_z) + potential(2 * index + 2, odd_y, odd_z)
                mid = potential(2 * index, odd_y, odd_z) + potential(2 * index + 1, odd_y, odd_z)
                rows.append(0.125 * low + 0.375 * mid)
            depth[odd_z] = 0.125 * (row_before(rows[1]) + row_after(rows[0])) + 0.375 * (rows[0] + rows[1])
        cells = 0.125 * (lane_before(depth[1]) + lane_after(depth[0])) + 0.375 * (depth[0] + depth[1])
        out[index] = cells[RIM : RIM + YB]


SMEM = pl.BlockSpec(memory_space=pltpu.SMEM)
VMEM = pl.BlockSpec(memory_space=pltpu.VMEM)
F32 = jnp.float32


def place_spheres(meta, blocks):
    rows = jax.ShapeDtypeStruct((3, 2, 2, WY, CZ), F32)
    return pl.pallas_call(
        place_kernel,
        out_shape=(jax.ShapeDtypeStruct((FX, 2, 2, WY, CZ), F32), rows, rows),
        in_specs=[SMEM, VMEM],
        out_specs=(VMEM, VMEM, VMEM),
        scratch_shapes=[pltpu.VMEM((2, 36, 80, 128), F32)],
        compiler_params=pltpu.CompilerParams(vmem_limit_bytes=32 * 2**20),
        name="place_spheres",
    )(meta, blocks)


def potential_of(place, own, core, chip, dots, dots_core, dots_chip):
    return pl.pallas_call(
        main_kernel,
        out_shape=jax.ShapeDtypeStruct((CX, YB, CZ), F32),
        in_specs=[SMEM] + [VMEM] * 6,
        out_specs=VMEM,
        scratch_shapes=[
            pltpu.VMEM((FX + 6, 2, 2, WY, CZ), F32),
            pltpu.VMEM((FX + 4, 2, 2, WY, CZ), F32),
            pltpu.VMEM((FX + 2, 2, 2, WY, CZ), F32),
        ],
        compiler_params=pltpu.CompilerParams(vmem_limit_bytes=32 * 2**20),
        name="potential_of",
    )(place, own, core, chip, dots, dots_core, dots_chip)


def body(partial_density, moments, shape_functions, sphere_offsets, owned_count):
    slab = lax.axis_index("dom")
    part = lax.axis_index("band")
    slabs = lax.axis_size("dom")
    even_slab = lax.rem(slab, 2) == 0
    core_pairs = [(i, i ^ 1) for i in range(slabs)]
    chip_pairs = [(i, i + 1) for i in range(1, slabs - 1, 2)]
    chip_pairs = chip_pairs + [(j, i) for i, j in chip_pairs]

    live = jnp.arange(SLOTS) < owned_count[0]
    blocks = jnp.einsum(
        "ls,slk->sk",
        moments * live.astype(jnp.bfloat16)[None, :],
        shape_functions,
        preferred_element_type=F32,
    )
    offsets = jnp.stack(
        [sphere_offsets[0], jnp.where(live, sphere_offsets[1], FAR), sphere_offsets[2]]
    )
    packed = jnp.concatenate(
        [blocks, jnp.pad(offsets.T.astype(F32), ((0, 0), (0, 125)))], axis=1
    )
    before = lax.ppermute(packed, "dom", [(i, i + 1) for i in range(slabs - 1)])

    padded = jnp.pad(partial_density[0], ((0, 0), (RIM, RIM), (0, 0)))
    windows = jnp.stack([padded[:, YB * b : YB * b + WY] for b in range(PARTS)])
    own = lax.all_to_all(windows, "band", 0, 0).sum(0)

    size = SBX * SBY * SBZ
    cubes = jnp.concatenate([blocks, before[:, :size]]).reshape(2 * SLOTS, SBX, SBY, SBZ)
    cubes = jnp.pad(cubes, ((0, 0), (0, 0), (0, 32 - SBY), (0, 128 - SBZ)))
    before_offsets = before[:, size : size + 3].T.astype(jnp.int32)
    meta = jnp.concatenate(
        [
            offsets.reshape(-1),
            before_offsets.reshape(-1),
            (2 * YB * part - 2 * RIM)[None].astype(jnp.int32),
            lax.rem(slab, 2)[None].astype(jnp.int32),
        ]
    )
    dots, send_core, send_chip = place_spheres(meta, cubes)
    dots_core = lax.ppermute(send_core, "dom", core_pairs)
    dots_chip = lax.ppermute(send_chip, "dom", chip_pairs)

    core = lax.ppermute(jnp.where(even_slab, own[4:6], own[0:2]), "dom", core_pairs)
    chip = lax.ppermute(jnp.where(even_slab, own[0:2], own[4:6]), "dom", chip_pairs)
    place = jnp.stack([slab, part, jnp.int32(slabs - 1)]).astype(jnp.int32)
    result = potential_of(place, own, core, chip, dots, dots_core, dots_chip)
    copies = jnp.broadcast_to(result[None], (PARTS, CX, YB, CZ))
    gathered = lax.all_to_all(copies, "band", 0, 0)
    return gathered.transpose(1, 0, 2, 3).reshape(CX, PARTS * YB, CZ)


def solution(mesh):
    return jax.shard_map(
        body,
        mesh=mesh,
        in_specs=(
            P("band", "dom", None, None),
            P(None, "dom"),
            P("dom", None, None),
            P(None, "dom"),
            P("dom"),
        ),
        out_specs=P("dom", None, None),
        check_vma=False,
    )
```

```python
import jax
import jax.numpy as jnp
from jax import lax
from jax.experimental import pallas as pl
from jax.experimental.pallas import tpu as pltpu
from jax.sharding import PartitionSpec as P

SLOTS = 8
SBX = 12
SBY = 24
SBZ = 24
BLOCK = SBX * SBY * SBZ
NL = 9
TAIL = 2 * SBY * SBZ + 128
CX = 6
FX = 12
RIM = 2
PARTS = 8
YB = 12
WY = 16
CZ = 128
FAR = -4096

KAPPA = 0.804
MU = 0.2195
PREFACTOR = -0.75 * (3.0 / 3.141592653589793) ** (1.0 / 3.0)
SCALE = 4.0 * (3.0 * 3.141592653589793**2) ** (2.0 / 3.0)
HALF_INVERSE = 0.5 / 0.2
DAMP = MU / KAPPA * HALF_INVERSE**2 / SCALE
B0 = PREFACTOR * 4.0 / 3.0 * (1.0 + KAPPA)
B1 = PREFACTOR * -4.0 * KAPPA
B2 = PREFACTOR * 8.0 / 3.0 * KAPPA
FLUX = 2.0 * HALF_INVERSE**2 * PREFACTOR * MU / SCALE


def windows_kernel(cells, windows, held, sems):
    copies = []
    for third in range(3):
        planes = pl.ds(2 * third, 2)
        copies.append(pltpu.make_async_copy(cells.at[0, planes], held.at[planes], sems.at[third]))
        copies[-1].start()
    for third in range(3):
        copies[third].wait()
        planes = pl.ds(2 * third, 2)
        for part in range(PARTS):
            first = YB * part - RIM
            low, high = max(first, 0), min(first + WY, PARTS * YB)
            rows = held[planes, low:high, :]
            if low > first:
                rows = jnp.concatenate([jnp.zeros((2, low - first, CZ), jnp.float32), rows], axis=1)
            if high < first + WY:
                rows = jnp.concatenate([rows, jnp.zeros((2, first + WY - high, CZ), jnp.float32)], axis=1)
            windows[part, planes] = rows


def blocks_kernel(offsets, count, moments, shapes, packed, tail, held, sems):
    step = BLOCK // 3
    copies = []
    for third in range(3):
        lanes = pl.ds(step * third, step)
        copies.append(
            pltpu.make_async_copy(shapes.at[:, :, lanes], held.at[:, :, lanes], sems.at[third])
        )
        copies[-1].start()
    row = lax.broadcasted_iota(jnp.int32, (SLOTS, 128), 0)
    lane = lax.broadcasted_iota(jnp.int32, (SLOTS, 128), 1)
    info = jnp.zeros((SLOTS, 128), jnp.int32)
    for which in range(SLOTS):
        for dim in range(3):
            value = offsets[dim, which]
            if dim == 1:
                value = jnp.where(which < count[0], value, FAR)
            info = jnp.where((row == which) & (lane == dim), value, info)
    packed[:, BLOCK : BLOCK + 128] = info.astype(jnp.float32)
    slot = lax.broadcasted_iota(jnp.int32, (SLOTS, 1), 0)
    weights = jnp.where(slot < count[0], moments[...].astype(jnp.float32), 0.0)
    for third in range(3):
        copies[third].wait()
        for chunk in range(3):
            lanes = pl.ds(step * third + chunk * (step // 3), step // 3)
            total = weights[:, 0:1] * held[0, :, lanes].astype(jnp.float32)
            for channel in range(1, NL):
                total = total + weights[:, channel : channel + 1] * held[channel, :, lanes].astype(
                    jnp.float32
                )
            packed[:, lanes] = total
    tail[...] = packed[:, BLOCK + 128 - TAIL :]


def spread_blocks(sources, flat, total):
    lane = lax.broadcasted_iota(jnp.int32, (SLOTS, 128), 1)
    for read, depth_x, _, begin, _, _ in sources:
        tiles = {}
        for line in range(depth_x * SBY):
            tile, skip = divmod(line * SBZ, 128)
            for needed in (tile, tile + 1) if skip + SBZ > 128 else (tile,):
                if needed not in tiles:
                    tiles = {k: v for k, v in tiles.items() if k >= tile}
                    tiles[needed] = read(needed)
            cells = tiles[tile]
            if skip + SBZ > 128:
                cells = jnp.where(lane >= skip, cells, tiles[tile + 1])
            if skip:
                cells = pltpu.roll(cells, 128 - skip, 1)
            flat[pl.ds(64 + SLOTS * (begin * SBY + line), SLOTS), :] = jnp.where(lane < SBZ, cells, 0.0)
    column = lax.broadcasted_iota(jnp.int32, (128, 256), 1)
    fine_z = jnp.where(column < 128, 2 * column, 2 * column - 255)
    inner_z = fine_z - lax.broadcasted_iota(jnp.int32, (128, 256), 0)
    row_z = lax.broadcasted_iota(jnp.int32, (128, 256), 0) < SBZ
    row_y = lax.broadcasted_iota(jnp.int32, (32, 128), 0)
    first_row = 2 * (YB * lax.axis_index("band") - RIM)
    for _, depth_x, first_plane, begin, value, there in sources:

        def one(slot, carry):
            row = value(slot, 0)
            col = value(slot, 1) - first_row + 24
            depth = value(slot, 2)
            meets = (col > 0) & (col < 56)

            @pl.when(meets if there is None else meets & there)
            def _():
                shift = lax.rem(col, 8)
                base = pl.multiple_of(col - shift, 8)
                held = (row_y >= shift) & (row_y < shift + SBY)
                parts = []
                for x in range(depth_x):
                    start = 64 + ((begin + x) * SBY - shift) * SLOTS + slot
                    parts.append(jnp.where(held, flat[pl.ds(start, 32, stride=SLOTS), :], 0.0))
                block = jnp.concatenate(parts, axis=0)
                high = block.astype(jnp.bfloat16)
                low = (block - high.astype(jnp.float32)).astype(jnp.bfloat16)
                pick = jnp.where((inner_z == depth) & row_z, 1.0, 0.0).astype(jnp.bfloat16)
                spread = jnp.dot(high, pick, preferred_element_type=jnp.float32)
                spread = spread + jnp.dot(low, pick, preferred_element_type=jnp.float32)
                planes = pl.ds(row + first_plane, depth_x)
                rows = pl.ds(base, 32)
                spread = spread.reshape(depth_x, 32, 256)
                for odd_z in range(2):
                    half = spread[:, :, 128 * odd_z : 128 * odd_z + 128]
                    total[odd_z, planes, rows, :] = total[odd_z, planes, rows, :] + half

            return carry

        lax.fori_loop(0, SLOTS, one, 0)


def place_own_kernel(offsets, count, own, out, flat, total):
    for odd_z in range(2):
        total[odd_z, pl.ds(11, 18), pl.ds(24, 32), :] = jnp.zeros((18, 32, 128), jnp.float32)

    def read(tile):
        return own[:, 128 * tile : 128 * tile + 128]

    def value(slot, which):
        if which == 1:
            return jnp.where(slot < count[0], offsets[1, slot], FAR)
        return offsets[which, slot]

    spread_blocks([(read, SBX, 14, 0, value, None)], flat, total)
    for odd_z in range(2):
        out[odd_z] = total[odd_z, pl.ds(11, 18), pl.ds(24, 32), :]


def place_kernel(own, core, chip, second, out, flat, total, info, sems):
    slab = lax.axis_index("dom")
    even_slab = lax.rem(slab, 2) == 0
    copies = []
    for index, (ref, start) in enumerate(
        ((core, BLOCK), (chip, BLOCK), (second, TAIL - 128))
    ):
        copies.append(
            pltpu.make_async_copy(ref.at[:, pl.ds(start, 128)], info.at[index], sems.at[index])
        )
        copies[-1].start()
    for odd_z in range(2):
        total[odd_z, pl.ds(11, 18), pl.ds(24, 32), :] = own[odd_z]

    def before_tile(tile):
        lanes = pl.ds(128 * tile, 128)
        return jnp.where(even_slab, chip[:, lanes], core[:, lanes])

    def after_tile(tile):
        lanes = pl.ds(128 * tile, 128)
        return jnp.where(even_slab, core[:, lanes], chip[:, lanes])

    def second_tile(tile):
        return second[:, 128 * tile : 128 * tile + 128]

    def value_of(if_even, if_odd):
        def value(slot, which):
            both = jnp.where(even_slab, info[if_even, slot, which], info[if_odd, slot, which])
            return both.astype(jnp.int32)

        return value

    for copy in copies:
        copy.wait()
    last = lax.axis_size("dom") - 1
    spread_blocks(
        [
            (before_tile, SBX, 2, 0, value_of(1, 0), slab > 0),
            (after_tile, 3, 26, SBX, value_of(0, 1), slab < last),
            (second_tile, 2, 0, SBX + 3, value_of(2, 2), slab > 1),
        ],
        flat,
        total,
    )
    for plane in range(FX + 6):
        for odd_y in range(2):
            for odd_z in range(2):
                rows = pl.ds(24 + odd_y, WY, stride=2)
                out[plane, odd_y, odd_z] = total[odd_z, plane + 11, rows, :]


def own_kernel(windows, own, send_core, send_chip):
    for plane in range(CX):
        cells = windows[0, plane]
        for part in range(1, PARTS):
            cells = cells + windows[part, plane]
        own[plane] = cells
    even_slab = lax.rem(lax.axis_index("dom"), 2) == 0
    send_core[...] = jnp.where(even_slab, own[CX - 2 : CX], own[0:2])
    send_chip[...] = jnp.where(even_slab, own[0:2], own[CX - 2 : CX])


def main_kernel(own, core, chip, dots, out, dens, flux_x, value):
    slab = lax.axis_index("dom")
    part = lax.axis_index("band")
    last = lax.axis_size("dom") - 1
    even_slab = lax.rem(slab, 2) == 0
    lane = lax.broadcasted_iota(jnp.int32, (WY, CZ), 1)
    first_lane = lane == 0
    last_lane = lane == CZ - 1
    row = lax.broadcasted_iota(jnp.int32, (WY, CZ), 0) + (YB * part - RIM)
    inside = (row >= 0) & (row < PARTS * YB)

    def row_before(x):
        return pltpu.roll(x, 1, 0)

    def row_after(x):
        return pltpu.roll(x, WY - 1, 0)

    def lane_before(x):
        return jnp.where(first_lane, 0.0, pltpu.roll(x, 1, 1))

    def lane_after(x):
        return jnp.where(last_lane, 0.0, pltpu.roll(x, CZ - 1, 1))

    def coarse(index):
        if index < 0:
            cells = jnp.where(even_slab, chip[index + 2], core[index + 2])
            return jnp.where(slab > 0, cells, 0.0)
        if index >= CX:
            cells = jnp.where(even_slab, core[index - CX], chip[index - CX])
            return jnp.where(slab < last, cells, 0.0)
        return own[index]

    def spread(cells):
        middle = 0.75 * cells
        rows = [middle + 0.25 * row_before(cells), middle + 0.25 * row_after(cells)]
        result = []
        for cells_y in rows:
            middle = 0.75 * cells_y
            result.append(
                [middle + 0.25 * lane_before(cells_y), middle + 0.25 * lane_after(cells_y)]
            )
        return result

    def in_grid(plane):
        if plane < 0:
            return slab > 0
        if plane >= FX:
            return slab < last
        return None

    grids = {}
    for plane in range(-3, FX + 3):
        index, odd = plane // 2, plane % 2
        near = index + (1 if odd else -1)
        for which in (index, near):
            if which not in grids:
                grids[which] = spread(coarse(which))
        for old in [k for k in grids if k < min(index, near) - 1]:
            del grids[old]
        there = in_grid(plane)
        ok = inside if there is None else inside & there
        for odd_y in range(2):
            for odd_z in range(2):
                cells = 0.75 * grids[index][odd_y][odd_z] + 0.25 * grids[near][odd_y][odd_z]
                cells = cells + dots[plane + 3, odd_y, odd_z]
                dens[plane + 3, odd_y, odd_z] = jnp.where(ok, cells, 0.0)

    def density(plane):
        return [[dens[plane + 3, odd_y, odd_z] for odd_z in range(2)] for odd_y in range(2)]

    def differences(field_y, field_z):
        along_y = [[None] * 2 for _ in range(2)]
        along_z = [[None] * 2 for _ in range(2)]
        for other in range(2):
            along_y[0][other] = field_y[1][other] - row_before(field_y[1][other])
            along_y[1][other] = row_after(field_y[0][other]) - field_y[0][other]
            along_z[other][0] = field_z[other][1] - lane_before(field_z[other][1])
            along_z[other][1] = lane_after(field_z[other][0]) - field_z[other][0]
        return along_y, along_z

    def store_flux(plane):
        there = in_grid(plane)
        ok = inside if there is None else inside & there
        here = density(plane)
        grad_y, grad_z = differences(here, here)
        flux_y = [[None] * 2 for _ in range(2)]
        flux_z = [[None] * 2 for _ in range(2)]
        by_density = [[None] * 2 for _ in range(2)]
        for odd_y in range(2):
            for odd_z in range(2):
                grad_x = dens[plane + 4, odd_y, odd_z] - dens[plane + 2, odd_y, odd_z]
                gy, gz = grad_y[odd_y][odd_z], grad_z[odd_y][odd_z]
                squared = grad_x * grad_x + gy * gy + gz * gz
                cells = jnp.where(ok, here[odd_y][odd_z], 1.0)
                inverse_root = jnp.exp(jnp.log(cells) * (-1.0 / 3.0))
                power_2 = inverse_root * inverse_root
                power_4 = power_2 * power_2
                inverse = 1.0 / (1.0 + DAMP * squared * (power_4 * power_4))
                by_density[odd_y][odd_z] = cells * power_2 * (B0 + inverse * (B1 + B2 * inverse))
                weight = jnp.where(ok, FLUX * power_4 * (inverse * inverse), 0.0)
                flux_x[plane + 2, odd_y, odd_z] = weight * grad_x
                flux_y[odd_y][odd_z] = weight * gy
                flux_z[odd_y][odd_z] = weight * gz
        if -1 <= plane <= FX:
            spread_y, spread_z = differences(flux_y, flux_z)
            for odd_y in range(2):
                for odd_z in range(2):
                    value[plane + 1, odd_y, odd_z] = by_density[odd_y][odd_z] - (
                        spread_y[odd_y][odd_z] + spread_z[odd_y][odd_z]
                    )

    for plane in range(-2, FX + 2):
        store_flux(plane)

    def potential(plane, odd_y, odd_z):
        there = in_grid(plane)
        ok = inside if there is None else inside & there
        cells = value[plane + 1, odd_y, odd_z] - (
            flux_x[plane + 3, odd_y, odd_z] - flux_x[plane + 1, odd_y, odd_z]
        )
        return jnp.where(ok, cells, 0.0)

    for index in range(CX):
        depth = [None, None]
        for odd_z in range(2):
            rows = []
            for odd_y in range(2):
                low = potential(2 * index - 1, odd_y, odd_z) + potential(2 * index + 2, odd_y, odd_z)
                mid = potential(2 * index, odd_y, odd_z) + potential(2 * index + 1, odd_y, odd_z)
                rows.append(0.125 * low + 0.375 * mid)
            depth[odd_z] = 0.125 * (row_before(rows[1]) + row_after(rows[0])) + 0.375 * (rows[0] + rows[1])
        cells = 0.125 * (lane_before(depth[1]) + lane_after(depth[0])) + 0.375 * (depth[0] + depth[1])
        for copy in range(PARTS):
            out[copy, index] = cells[RIM : RIM + YB]


SMEM = pl.BlockSpec(memory_space=pltpu.SMEM)
VMEM = pl.BlockSpec(memory_space=pltpu.VMEM)
HBM = pl.BlockSpec(memory_space=pltpu.HBM)
ANY = pl.BlockSpec(memory_space=pl.ANY)
F32 = jnp.float32


def is_dims(x):
    return isinstance(x, tuple) and all(isinstance(n, int) for n in x)


def call(kernel, name, out, in_specs, scratch=()):
    shapes = jax.tree.map(lambda dims: jax.ShapeDtypeStruct(dims, F32), out, is_leaf=is_dims)
    return pl.pallas_call(
        kernel,
        out_shape=shapes,
        in_specs=in_specs,
        out_specs=jax.tree.map(lambda dims: VMEM, out, is_leaf=is_dims),
        scratch_shapes=list(scratch),
        compiler_params=pltpu.CompilerParams(vmem_limit_bytes=32 * 2**20),
        name=name,
    )


def body(partial_density, moments, shape_functions, sphere_offsets, owned_count):
    slabs = lax.axis_size("dom")
    core_pairs = [(i, i ^ 1) for i in range(slabs)]
    second = [(i, (i + 2) % slabs) for i in range(slabs)]
    chip_pairs = []
    for b in range(PARTS):
        for i in range(slabs):
            j = i + 1 if i % 2 else i - 1
            there = (b, j) if 0 <= j < slabs else (b ^ 1, i)
            chip_pairs.append((b * slabs + i, there[0] * slabs + there[1]))

    total = pltpu.VMEM((2, 41, 80, 128), F32)
    windows = call(
        windows_kernel,
        "windows",
        (PARTS, CX, WY, CZ),
        [HBM],
        [pltpu.VMEM((CX, PARTS * YB, CZ), F32), pltpu.SemaphoreType.DMA((3,))],
    )(partial_density)
    windows = lax.all_to_all(windows, "band", 0, 0)

    packed, tail = call(
        blocks_kernel,
        "blocks",
        ((SLOTS, BLOCK + 128), (SLOTS, TAIL)),
        [SMEM, SMEM, VMEM, HBM],
        [pltpu.VMEM((NL, SLOTS, BLOCK), jnp.bfloat16), pltpu.SemaphoreType.DMA((3,))],
    )(sphere_offsets, owned_count, moments.T, shape_functions.transpose(1, 0, 2))
    dots_core = lax.ppermute(packed, "dom", core_pairs)
    dots_second = lax.ppermute(tail, "dom", second)
    dots_chip = lax.ppermute(packed, ("band", "dom"), chip_pairs)

    own, send_core, send_chip = call(
        own_kernel, "own_window", ((CX, WY, CZ), (2, WY, CZ), (2, WY, CZ)), [VMEM]
    )(windows)
    dots = call(
        place_own_kernel,
        "place_own",
        (2, FX + 6, 32, CZ),
        [SMEM, SMEM, VMEM],
        [pltpu.VMEM((64 + SLOTS * SBX * SBY + 128, 128), F32), total],
    )(sphere_offsets, owned_count, packed)
    core = lax.ppermute(send_core, "dom", core_pairs)
    chip = lax.ppermute(send_chip, ("band", "dom"), chip_pairs)

    dots = call(
        place_kernel,
        "place_others",
        (FX + 6, 2, 2, WY, CZ),
        [VMEM] * 4,
        [
            pltpu.VMEM((64 + SLOTS * (SBX + 5) * SBY + 128, 128), F32),
            total,
            pltpu.SMEM((3, SLOTS, 128), F32),
            pltpu.SemaphoreType.DMA((3,)),
        ],
    )(dots, dots_core, dots_chip, dots_second)
    result = call(
        main_kernel,
        "potential_of",
        (PARTS, CX, YB, CZ),
        [VMEM] * 4,
        [
            pltpu.VMEM((FX + 6, 2, 2, WY, CZ), F32),
            pltpu.VMEM((FX + 4, 2, 2, WY, CZ), F32),
            pltpu.VMEM((FX + 2, 2, 2, WY, CZ), F32),
        ],
    )(own, core, chip, dots)
    gathered = lax.all_to_all(result, "band", 0, 0)
    return gathered.transpose(1, 0, 2, 3).reshape(CX, PARTS * YB, CZ)


def solution(mesh):
    return jax.shard_map(
        body,
        mesh=mesh,
        in_specs=(
            P("band", "dom", None, None),
            P(None, "dom"),
            P("dom", None, None),
            P(None, "dom"),
            P("dom"),
        ),
        out_specs=P("dom", None, None),
        check_vma=False,
    )
```

```python
import jax
import jax.numpy as jnp
from jax import lax
from jax.experimental import pallas as pl
from jax.experimental.pallas import tpu as pltpu
from jax.sharding import PartitionSpec as P

SLOTS = 8
SBX = 12
SBY = 24
SBZ = 24
BLOCK = SBX * SBY * SBZ
NL = 9
TAIL = 2 * SBY * SBZ + 128
CX = 6
FX = 12
RIM = 2
PARTS = 8
YB = 12
WY = 16
CZ = 128
FAR = -4096

KAPPA = 0.804
MU = 0.2195
PREFACTOR = -0.75 * (3.0 / 3.141592653589793) ** (1.0 / 3.0)
SCALE = 4.0 * (3.0 * 3.141592653589793**2) ** (2.0 / 3.0)
HALF_INVERSE = 0.5 / 0.2
DAMP = MU / KAPPA * HALF_INVERSE**2 / SCALE
B0 = PREFACTOR * 4.0 / 3.0 * (1.0 + KAPPA)
B1 = PREFACTOR * -4.0 * KAPPA
B2 = PREFACTOR * 8.0 / 3.0 * KAPPA
FLUX = 2.0 * HALF_INVERSE**2 * PREFACTOR * MU / SCALE


def windows_kernel(cells, windows):
    for part in range(PARTS):
        first = YB * part - RIM
        low, high = max(first, 0), min(first + WY, PARTS * YB)
        rows = cells[0, :, low:high, :]
        if low > first:
            rows = jnp.concatenate([jnp.zeros((CX, low - first, CZ), jnp.float32), rows], axis=1)
        if high < first + WY:
            rows = jnp.concatenate([rows, jnp.zeros((CX, first + WY - high, CZ), jnp.float32)], axis=1)
        windows[part] = rows


def blocks_kernel(offsets, count, moments, shapes, packed, tail):
    row = lax.broadcasted_iota(jnp.int32, (SLOTS, SLOTS), 0)
    lane = lax.broadcasted_iota(jnp.int32, (SLOTS, SLOTS), 1)
    slot = lax.broadcasted_iota(jnp.int32, (SLOTS, 1), 0)
    alive = slot < count[...]
    where = lax.broadcasted_iota(jnp.int32, (SLOTS, 128), 1)
    info = jnp.zeros((SLOTS, 128), jnp.float32)
    for dim in range(3):
        values = jnp.broadcast_to(offsets[dim : dim + 1, :], (SLOTS, SLOTS)).astype(jnp.float32)
        column = jnp.sum(jnp.where(row == lane, values, 0.0), axis=1, keepdims=True)
        if dim == 1:
            column = jnp.where(alive, column, float(FAR))
        info = jnp.where(where == dim, column, info)
    packed[:, BLOCK : BLOCK + 128] = info
    weights = jnp.where(alive, moments[...].astype(jnp.float32), 0.0)
    step = BLOCK // 9
    for chunk in range(9):
        lanes = pl.ds(chunk * step, step)
        total = weights[:, 0:1] * shapes[0, :, lanes].astype(jnp.float32)
        for channel in range(1, NL):
            total = total + weights[:, channel : channel + 1] * shapes[channel, :, lanes].astype(
                jnp.float32
            )
        packed[:, lanes] = total
    tail[...] = packed[:, BLOCK + 128 - TAIL :]


def line_up(read, depth_x, begin, flat):
    lane = lax.broadcasted_iota(jnp.int32, (SLOTS, 128), 1)
    tiles = {}
    for line in range(depth_x * SBY):
        tile, skip = divmod(line * SBZ, 128)
        for needed in (tile, tile + 1) if skip + SBZ > 128 else (tile,):
            if needed not in tiles:
                tiles = {k: v for k, v in tiles.items() if k >= tile}
                tiles[needed] = read(needed)
        cells = tiles[tile]
        if skip + SBZ > 128:
            cells = jnp.where(lane >= skip, cells, tiles[tile + 1])
        if skip:
            cells = pltpu.roll(cells, 128 - skip, 1)
        flat[pl.ds(64 + SLOTS * (begin * SBY + line), SLOTS), :] = jnp.where(lane < SBZ, cells, 0.0)


def whole_offsets(offsets, counts):
    lane = lax.broadcasted_iota(jnp.int32, (SLOTS, 128), 1)
    whole = offsets.astype(jnp.int32)
    row = jnp.max(jnp.where(lane == 0, whole, 0), axis=1, keepdims=True)
    there = whole - 2 * (YB * lax.axis_index("band") - RIM) + 24
    return jnp.where(lane == 1, jnp.where(counts(row), there, FAR), whole)


def spread_blocks(sources, flat, total, info):
    column = lax.broadcasted_iota(jnp.int32, (256, 256), 1)
    line = lax.rem(lax.broadcasted_iota(jnp.int32, (256, 256), 0), 128)
    inner_z = jnp.where(column < 128, 2 * column, 2 * column - 255) - line
    inner_z = jnp.where(line < SBZ, inner_z, -1)
    row_y = lax.broadcasted_iota(jnp.int32, (32, 128), 0)
    for which, (depth_x, first_plane, begin) in enumerate(sources):

        def one(slot, carry):
            col = info[which, slot, 1]

            @pl.when((col > 0) & (col < 56))
            def _():
                row = info[which, slot, 0]
                depth = info[which, slot, 2]
                shift = lax.rem(col, 8)
                base = pl.multiple_of(col - shift, 8)
                held = (row_y >= shift) & (row_y < shift + SBY)
                parts = []
                for x in range(depth_x):
                    start = 64 + ((begin + x) * SBY - shift) * SLOTS + slot
                    parts.append(jnp.where(held, flat[pl.ds(start, 32, stride=SLOTS), :], 0.0))
                block = jnp.concatenate(parts, axis=0)
                high = block.astype(jnp.bfloat16)
                low = (block - high.astype(jnp.float32)).astype(jnp.bfloat16)
                pick = jnp.where(inner_z == depth, 1.0, 0.0).astype(jnp.bfloat16)
                both = jnp.concatenate([high, low], axis=1)
                spread = jnp.dot(both, pick, preferred_element_type=jnp.float32)
                planes = pl.ds(row + first_plane, depth_x)
                rows = pl.ds(base, 32)
                spread = spread.reshape(depth_x, 32, 256)
                for odd_z in range(2):
                    half = spread[:, :, 128 * odd_z : 128 * odd_z + 128]
                    total[odd_z, planes, rows, :] = total[odd_z, planes, rows, :] + half

            return carry

        lax.fori_loop(0, SLOTS, one, 0)


def place_kernel(own, core, chip, out, flat, total, whole, info, sem):
    slab = lax.axis_index("dom")
    even_slab = lax.rem(slab, 2) == 0
    last = lax.axis_size("dom") - 1
    lanes = pl.ds(BLOCK, 128)
    before = jnp.where(even_slab, chip[:, lanes], core[:, lanes])
    after = jnp.where(even_slab, core[:, lanes], chip[:, lanes])
    whole[0] = whole_offsets(own[:, lanes], lambda row: row >= 0)
    whole[1] = whole_offsets(before, lambda row: (row >= 0) & (slab > 0))
    whole[2] = whole_offsets(after, lambda row: (row < 3) & (slab < last))
    copy = pltpu.make_async_copy(whole, info, sem)
    copy.start()
    for odd_z in range(2):
        total[odd_z, pl.ds(11, 18), pl.ds(24, 32), :] = jnp.zeros((18, 32, 128), jnp.float32)

    def own_tile(tile):
        return own[:, 128 * tile : 128 * tile + 128]

    def before_tile(tile):
        lanes = pl.ds(128 * tile, 128)
        return jnp.where(even_slab, chip[:, lanes], core[:, lanes])

    def after_tile(tile):
        lanes = pl.ds(128 * tile, 128)
        return jnp.where(even_slab, core[:, lanes], chip[:, lanes])

    line_up(own_tile, SBX, 0, flat)
    line_up(before_tile, SBX, SBX, flat)
    line_up(after_tile, 3, 2 * SBX, flat)
    copy.wait()
    spread_blocks([(SBX, 14, 0), (SBX, 2, SBX), (3, 26, 2 * SBX)], flat, total, info)
    for plane in range(FX + 6):
        for odd_y in range(2):
            for odd_z in range(2):
                rows = pl.ds(24 + odd_y, WY, stride=2)
                out[plane, odd_y, odd_z] = total[odd_z, plane + 11, rows, :]


def own_kernel(windows, own, send_core, send_chip):
    for plane in range(CX):
        cells = windows[0, plane]
        for part in range(1, PARTS):
            cells = cells + windows[part, plane]
        own[plane] = cells
    even_slab = lax.rem(lax.axis_index("dom"), 2) == 0
    send_core[...] = jnp.where(even_slab, own[CX - 2 : CX], own[0:2])
    send_chip[0:2] = jnp.where(even_slab, own[0:2], own[CX - 2 : CX])
    send_chip[2:4] = own[2:4]


def main_kernel(own, core, chip, dots, second, out, dens, flux_x, value, flat, total, whole, info, sem):
    slab = lax.axis_index("dom")
    part = lax.axis_index("band")
    last = lax.axis_size("dom") - 1
    even_slab = lax.rem(slab, 2) == 0
    whole[0] = whole_offsets(second[:, pl.ds(TAIL - 128, 128)], lambda row: (row >= 10) & (slab > 1))
    copy = pltpu.make_async_copy(whole, info, sem)
    copy.start()
    for odd_z in range(2):
        total[odd_z, pl.ds(0, 4), pl.ds(24, 32), :] = jnp.zeros((4, 32, CZ), jnp.float32)
    line_up(lambda tile: second[:, 128 * tile : 128 * tile + 128], 2, 0, flat)
    lane = lax.broadcasted_iota(jnp.int32, (WY, CZ), 1)
    first_lane = lane == 0
    last_lane = lane == CZ - 1
    row = lax.broadcasted_iota(jnp.int32, (WY, CZ), 0) + (YB * part - RIM)
    inside = (row >= 0) & (row < PARTS * YB)

    def row_before(x):
        return pltpu.roll(x, 1, 0)

    def row_after(x):
        return pltpu.roll(x, WY - 1, 0)

    def lane_before(x):
        return jnp.where(first_lane, 0.0, pltpu.roll(x, 1, 1))

    def lane_after(x):
        return jnp.where(last_lane, 0.0, pltpu.roll(x, CZ - 1, 1))

    def coarse(index):
        if index < 0:
            cells = jnp.where(even_slab, chip[index + 2], core[index + 2])
            return jnp.where(slab > 0, cells, 0.0)
        if index >= CX:
            cells = jnp.where(even_slab, core[index - CX], chip[index - CX])
            return jnp.where(slab < last, cells, 0.0)
        return own[index]

    def spread(cells):
        middle = 0.75 * cells
        rows = [middle + 0.25 * row_before(cells), middle + 0.25 * row_after(cells)]
        result = []
        for cells_y in rows:
            middle = 0.75 * cells_y
            result.append(
                [middle + 0.25 * lane_before(cells_y), middle + 0.25 * lane_after(cells_y)]
            )
        return result

    def in_grid(plane):
        if plane < 0:
            return slab > 0
        if plane >= FX:
            return slab < last
        return None

    copy.wait()
    spread_blocks([(2, -10, 0)], flat, total, info)

    grids = {}
    for plane in range(-3, FX + 3):
        index, odd = plane // 2, plane % 2
        near = index + (1 if odd else -1)
        for which in (index, near):
            if which not in grids:
                grids[which] = spread(coarse(which))
        for old in [k for k in grids if k < min(index, near) - 1]:
            del grids[old]
        there = in_grid(plane)
        ok = inside if there is None else inside & there
        for odd_y in range(2):
            for odd_z in range(2):
                cells = 0.75 * grids[index][odd_y][odd_z] + 0.25 * grids[near][odd_y][odd_z]
                cells = cells + dots[plane + 3, odd_y, odd_z]
                if plane < -1:
                    cells = cells + total[odd_z, plane + 4, pl.ds(24 + odd_y, WY, stride=2), :]
                dens[plane + 3, odd_y, odd_z] = jnp.where(ok, cells, 0.0)

    def density(plane):
        return [[dens[plane + 3, odd_y, odd_z] for odd_z in range(2)] for odd_y in range(2)]

    def differences(field_y, field_z):
        along_y = [[None] * 2 for _ in range(2)]
        along_z = [[None] * 2 for _ in range(2)]
        for other in range(2):
            along_y[0][other] = field_y[1][other] - row_before(field_y[1][other])
            along_y[1][other] = row_after(field_y[0][other]) - field_y[0][other]
            along_z[other][0] = field_z[other][1] - lane_before(field_z[other][1])
            along_z[other][1] = lane_after(field_z[other][0]) - field_z[other][0]
        return along_y, along_z

    def store_flux(plane):
        there = in_grid(plane)
        ok = inside if there is None else inside & there
        here = density(plane)
        grad_y, grad_z = differences(here, here)
        flux_y = [[None] * 2 for _ in range(2)]
        flux_z = [[None] * 2 for _ in range(2)]
        by_density = [[None] * 2 for _ in range(2)]
        for odd_y in range(2):
            for odd_z in range(2):
                grad_x = dens[plane + 4, odd_y, odd_z] - dens[plane + 2, odd_y, odd_z]
                gy, gz = grad_y[odd_y][odd_z], grad_z[odd_y][odd_z]
                squared = grad_x * grad_x + gy * gy + gz * gz
                cells = jnp.where(ok, here[odd_y][odd_z], 1.0)
                inverse_root = jnp.exp(jnp.log(cells) * (-1.0 / 3.0))
                power_2 = inverse_root * inverse_root
                power_4 = power_2 * power_2
                inverse = 1.0 / (1.0 + DAMP * squared * (power_4 * power_4))
                by_density[odd_y][odd_z] = cells * power_2 * (B0 + inverse * (B1 + B2 * inverse))
                weight = jnp.where(ok, FLUX * power_4 * (inverse * inverse), 0.0)
                flux_x[plane + 2, odd_y, odd_z] = weight * grad_x
                flux_y[odd_y][odd_z] = weight * gy
                flux_z[odd_y][odd_z] = weight * gz
        if -1 <= plane <= FX:
            spread_y, spread_z = differences(flux_y, flux_z)
            for odd_y in range(2):
                for odd_z in range(2):
                    value[plane + 1, odd_y, odd_z] = by_density[odd_y][odd_z] - (
                        spread_y[odd_y][odd_z] + spread_z[odd_y][odd_z]
                    )

    for plane in range(-2, FX + 2):
        store_flux(plane)

    def potential(plane, odd_y, odd_z):
        there = in_grid(plane)
        ok = inside if there is None else inside & there
        cells = value[plane + 1, odd_y, odd_z] - (
            flux_x[plane + 3, odd_y, odd_z] - flux_x[plane + 1, odd_y, odd_z]
        )
        return jnp.where(ok, cells, 0.0)

    for index in range(CX):
        depth = [None, None]
        for odd_z in range(2):
            rows = []
            for odd_y in range(2):
                low = potential(2 * index - 1, odd_y, odd_z) + potential(2 * index + 2, odd_y, odd_z)
                mid = potential(2 * index, odd_y, odd_z) + potential(2 * index + 1, odd_y, odd_z)
                rows.append(0.125 * low + 0.375 * mid)
            depth[odd_z] = 0.125 * (row_before(rows[1]) + row_after(rows[0])) + 0.375 * (rows[0] + rows[1])
        cells = 0.125 * (lane_before(depth[1]) + lane_after(depth[0])) + 0.375 * (depth[0] + depth[1])
        for copy in range(PARTS):
            out[copy, index] = cells[RIM : RIM + YB]


SMEM = pl.BlockSpec(memory_space=pltpu.SMEM)
VMEM = pl.BlockSpec(memory_space=pltpu.VMEM)
F32 = jnp.float32


def is_dims(x):
    return isinstance(x, tuple) and all(isinstance(n, int) for n in x)


def call(kernel, name, out, in_specs, scratch=()):
    shapes = jax.tree.map(lambda dims: jax.ShapeDtypeStruct(dims, F32), out, is_leaf=is_dims)
    return pl.pallas_call(
        kernel,
        out_shape=shapes,
        in_specs=in_specs,
        out_specs=jax.tree.map(lambda dims: VMEM, out, is_leaf=is_dims),
        scratch_shapes=list(scratch),
        compiler_params=pltpu.CompilerParams(vmem_limit_bytes=32 * 2**20),
        name=name,
    )


def body(partial_density, moments, shape_functions, sphere_offsets, owned_count):
    slabs = lax.axis_size("dom")
    core_pairs = [(i, i ^ 1) for i in range(slabs)]
    second = [(i, (i + 2) % slabs) for i in range(slabs)]
    chip_pairs = []
    for b in range(PARTS):
        for i in range(slabs):
            j = i + 1 if i % 2 else i - 1
            there = (b, j) if 0 <= j < slabs else (b ^ 1, i)
            chip_pairs.append((b * slabs + i, there[0] * slabs + there[1]))

    windows = call(windows_kernel, "windows", (PARTS, CX, WY, CZ), [VMEM])(partial_density)
    windows = lax.all_to_all(windows, "band", 0, 0)

    packed, tail = call(
        blocks_kernel,
        "blocks",
        ((SLOTS, BLOCK + 128), (SLOTS, TAIL)),
        [VMEM] * 4,
    )(sphere_offsets, owned_count.reshape(1, 1), moments.T, shape_functions.transpose(1, 0, 2))
    dots_core = lax.ppermute(packed, "dom", core_pairs)
    dots_second = lax.ppermute(tail, "dom", second)
    dots_chip = lax.ppermute(packed, ("band", "dom"), chip_pairs)

    own, send_core, send_chip = call(
        own_kernel, "own_window", ((CX, WY, CZ), (2, WY, CZ), (4, WY, CZ)), [VMEM]
    )(windows)
    core = lax.ppermute(send_core, "dom", core_pairs)
    chip = lax.ppermute(send_chip, ("band", "dom"), chip_pairs)
    dots = call(
        place_kernel,
        "place_spheres",
        (FX + 6, 2, 2, WY, CZ),
        [VMEM] * 3,
        [
            pltpu.VMEM((64 + SLOTS * (2 * SBX + 3) * SBY + 128, 128), F32),
            pltpu.VMEM((2, 41, 80, CZ), F32),
            pltpu.VMEM((3, SLOTS, 128), jnp.int32),
            pltpu.SMEM((3, SLOTS, 128), jnp.int32),
            pltpu.SemaphoreType.DMA,
        ],
    )(packed, dots_core, dots_chip)
    result = call(
        main_kernel,
        "potential_of",
        (PARTS, CX, YB, CZ),
        [VMEM] * 5,
        [
            pltpu.VMEM((FX + 6, 2, 2, WY, CZ), F32),
            pltpu.VMEM((FX + 4, 2, 2, WY, CZ), F32),
            pltpu.VMEM((FX + 2, 2, 2, WY, CZ), F32),
            pltpu.VMEM((64 + SLOTS * 2 * SBY + 128, 128), F32),
            pltpu.VMEM((2, 4, 80, CZ), F32),
            pltpu.VMEM((1, SLOTS, 128), jnp.int32),
            pltpu.SMEM((1, SLOTS, 128), jnp.int32),
            pltpu.SemaphoreType.DMA,
        ],
    )(own, core, chip, dots, dots_second)
    gathered = lax.all_to_all(result, "band", 0, 0)
    return gathered.transpose(1, 0, 2, 3).reshape(CX, PARTS * YB, CZ)


def solution(mesh):
    return jax.shard_map(
        body,
        mesh=mesh,
        in_specs=(
            P("band", "dom", None, None),
            P(None, "dom"),
            P("dom", None, None),
            P(None, "dom"),
            P("dom"),
        ),
        out_specs=P("dom", None, None),
        check_vma=False,
    )
```

```python
import jax
import jax.numpy as jnp
from jax import lax
from jax.experimental import pallas as pl
from jax.experimental.pallas import tpu as pltpu
from jax.sharding import PartitionSpec as P

SLOTS = 8
SBX = 12
SBY = 24
SBZ = 24
BLOCK = SBX * SBY * SBZ
NL = 9
TAIL = 2 * SBY * SBZ + 128
CX = 6
FX = 12
RIM = 2
PARTS = 8
YB = 12
WY = 16
CZ = 128
FAR = -4096

KAPPA = 0.804
MU = 0.2195
PREFACTOR = -0.75 * (3.0 / 3.141592653589793) ** (1.0 / 3.0)
SCALE = 4.0 * (3.0 * 3.141592653589793**2) ** (2.0 / 3.0)
HALF_INVERSE = 0.5 / 0.2
DAMP = MU / KAPPA * HALF_INVERSE**2 / SCALE
B0 = PREFACTOR * 4.0 / 3.0 * (1.0 + KAPPA)
B1 = PREFACTOR * -4.0 * KAPPA
B2 = PREFACTOR * 8.0 / 3.0 * KAPPA
FLUX = 2.0 * HALF_INVERSE**2 * PREFACTOR * MU / SCALE


def windows_kernel(cells, windows):
    for part in range(PARTS):
        first = YB * part - RIM
        low, high = max(first, 0), min(first + WY, PARTS * YB)
        rows = cells[0, :, low:high, :]
        if low > first:
            rows = jnp.concatenate([jnp.zeros((CX, low - first, CZ), jnp.float32), rows], axis=1)
        if high < first + WY:
            rows = jnp.concatenate([rows, jnp.zeros((CX, first + WY - high, CZ), jnp.float32)], axis=1)
        windows[part] = rows


def blocks_kernel(offsets, count, moments, shapes, packed, tail):
    row = lax.broadcasted_iota(jnp.int32, (SLOTS, SLOTS), 0)
    lane = lax.broadcasted_iota(jnp.int32, (SLOTS, SLOTS), 1)
    slot = lax.broadcasted_iota(jnp.int32, (SLOTS, 1), 0)
    alive = slot < count[...]
    where = lax.broadcasted_iota(jnp.int32, (SLOTS, 128), 1)
    info = jnp.zeros((SLOTS, 128), jnp.float32)
    for dim in range(3):
        values = jnp.broadcast_to(offsets[dim : dim + 1, :], (SLOTS, SLOTS)).astype(jnp.float32)
        column = jnp.sum(jnp.where(row == lane, values, 0.0), axis=1, keepdims=True)
        if dim == 1:
            column = jnp.where(alive, column, float(FAR))
        info = jnp.where(where == dim, column, info)
    packed[:, BLOCK : BLOCK + 128] = info
    weights = jnp.where(alive, moments[...].astype(jnp.float32), 0.0)
    step = BLOCK // 9
    for chunk in range(9):
        lanes = pl.ds(chunk * step, step)
        total = weights[:, 0:1] * shapes[0, :, lanes].astype(jnp.float32)
        for channel in range(1, NL):
            total = total + weights[:, channel : channel + 1] * shapes[channel, :, lanes].astype(
                jnp.float32
            )
        packed[:, lanes] = total
    tail[...] = packed[:, BLOCK + 128 - TAIL :]


def line_up(read, depth_x, begin, flat):
    lane = lax.broadcasted_iota(jnp.int32, (SLOTS, 128), 1)
    tiles = {}
    for line in range(depth_x * SBY):
        tile, skip = divmod(line * SBZ, 128)
        for needed in (tile, tile + 1) if skip + SBZ > 128 else (tile,):
            if needed not in tiles:
                tiles = {k: v for k, v in tiles.items() if k >= tile}
                tiles[needed] = read(needed)
        cells = tiles[tile]
        if skip + SBZ > 128:
            cells = jnp.where(lane >= skip, cells, tiles[tile + 1])
        if skip:
            cells = pltpu.roll(cells, 128 - skip, 1)
        flat[pl.ds(64 + SLOTS * (begin * SBY + line), SLOTS), :] = jnp.where(lane < SBZ, cells, 0.0)


def whole_offsets(offsets, counts):
    lane = lax.broadcasted_iota(jnp.int32, (SLOTS, 128), 1)
    whole = offsets.astype(jnp.int32)
    row = jnp.max(jnp.where(lane == 0, whole, 0), axis=1, keepdims=True)
    there = whole - 2 * (YB * lax.axis_index("band") - RIM) + 24
    return jnp.where(lane == 1, jnp.where(counts(row), there, FAR), whole)


def spread_blocks(groups, flat, total, info, chosen):
    column = lax.broadcasted_iota(jnp.int32, (256, 256), 1)
    line = lax.rem(lax.broadcasted_iota(jnp.int32, (256, 256), 0), 128)
    inner_z = jnp.where(column < 128, 2 * column, 2 * column - 255) - line
    inner_z = jnp.where(line < SBZ, inner_z, -1)
    row_y = lax.broadcasted_iota(jnp.int32, (32, 128), 0)
    for first_source, sources, depth_x, first_plane, begin in groups:
        count = jnp.int32(0)
        for which in range(sources):
            for slot in range(SLOTS):
                col = info[first_source + which, slot, 1]
                chosen[count] = which * SLOTS + slot
                count = count + jnp.where((col > 0) & (col < 56), 1, 0)

        def one(index, carry):
            both = chosen[index]
            source = lax.shift_right_logical(both, 3)
            slot = both & (SLOTS - 1)
            row = info[first_source + source, slot, 0]
            col = info[first_source + source, slot, 1]
            depth = info[first_source + source, slot, 2]
            shift = lax.rem(col, 8)
            base = pl.multiple_of(col - shift, 8)
            held = (row_y >= shift) & (row_y < shift + SBY)
            origin = 64 + ((begin + SBX * source) * SBY - shift) * SLOTS + slot
            parts = []
            for x in range(depth_x):
                start = origin + x * SBY * SLOTS
                parts.append(jnp.where(held, flat[pl.ds(start, 32, stride=SLOTS), :], 0.0))
            block = jnp.concatenate(parts, axis=0)
            high = block.astype(jnp.bfloat16)
            low = (block - high.astype(jnp.float32)).astype(jnp.bfloat16)
            pick = jnp.where(inner_z == depth, 1.0, 0.0).astype(jnp.bfloat16)
            terms = jnp.concatenate([high, low], axis=1)
            spread = jnp.dot(terms, pick, preferred_element_type=jnp.float32)
            planes = pl.ds(row + first_plane - FX * source, depth_x)
            rows = pl.ds(base, 32)
            spread = spread.reshape(depth_x, 32, 256)
            for odd_z in range(2):
                half = spread[:, :, 128 * odd_z : 128 * odd_z + 128]
                total[odd_z, planes, rows, :] = total[odd_z, planes, rows, :] + half
            return carry

        lax.fori_loop(0, count, one, 0)


def place_kernel(own, core, chip, out, flat, total, whole, info, chosen, sem):
    slab = lax.axis_index("dom")
    even_slab = lax.rem(slab, 2) == 0
    last = lax.axis_size("dom") - 1
    lanes = pl.ds(BLOCK, 128)
    before = jnp.where(even_slab, chip[:, lanes], core[:, lanes])
    after = jnp.where(even_slab, core[:, lanes], chip[:, lanes])
    whole[0] = whole_offsets(own[:, lanes], lambda row: row >= 0)
    whole[1] = whole_offsets(before, lambda row: (row >= 0) & (slab > 0))
    whole[2] = whole_offsets(after, lambda row: (row < 3) & (slab < last))
    copy = pltpu.make_async_copy(whole, info, sem)
    copy.start()
    for odd_z in range(2):
        total[odd_z, pl.ds(11, 18), pl.ds(24, 32), :] = jnp.zeros((18, 32, 128), jnp.float32)

    def own_tile(tile):
        return own[:, 128 * tile : 128 * tile + 128]

    def before_tile(tile):
        lanes = pl.ds(128 * tile, 128)
        return jnp.where(even_slab, chip[:, lanes], core[:, lanes])

    def after_tile(tile):
        lanes = pl.ds(128 * tile, 128)
        return jnp.where(even_slab, core[:, lanes], chip[:, lanes])

    line_up(own_tile, SBX, 0, flat)
    line_up(before_tile, SBX, SBX, flat)
    line_up(after_tile, 3, 2 * SBX, flat)
    copy.wait()
    spread_blocks([(0, 2, SBX, 14, 0), (2, 1, 3, 26, 2 * SBX)], flat, total, info, chosen)
    for plane in range(FX + 6):
        for odd_y in range(2):
            for odd_z in range(2):
                rows = pl.ds(24 + odd_y, WY, stride=2)
                out[plane, odd_y, odd_z] = total[odd_z, plane + 11, rows, :]


def own_kernel(windows, own, send_core, send_chip):
    for plane in range(CX):
        cells = windows[0, plane]
        for part in range(1, PARTS):
            cells = cells + windows[part, plane]
        own[plane] = cells
    even_slab = lax.rem(lax.axis_index("dom"), 2) == 0
    send_core[...] = jnp.where(even_slab, own[CX - 2 : CX], own[0:2])
    send_chip[0:2] = jnp.where(even_slab, own[0:2], own[CX - 2 : CX])
    send_chip[2:4] = own[2:4]


def main_kernel(own, core, chip, dots, second, out, dens, flux_x, value, flat, total, whole, info, chosen, sem):
    slab = lax.axis_index("dom")
    part = lax.axis_index("band")
    last = lax.axis_size("dom") - 1
    even_slab = lax.rem(slab, 2) == 0
    whole[0] = whole_offsets(second[:, pl.ds(TAIL - 128, 128)], lambda row: (row >= 10) & (slab > 1))
    copy = pltpu.make_async_copy(whole, info, sem)
    copy.start()
    for odd_z in range(2):
        total[odd_z, pl.ds(0, 4), pl.ds(24, 32), :] = jnp.zeros((4, 32, CZ), jnp.float32)
    line_up(lambda tile: second[:, 128 * tile : 128 * tile + 128], 2, 0, flat)
    lane = lax.broadcasted_iota(jnp.int32, (WY, CZ), 1)
    first_lane = lane == 0
    last_lane = lane == CZ - 1
    row = lax.broadcasted_iota(jnp.int32, (WY, CZ), 0) + (YB * part - RIM)
    inside = (row >= 0) & (row < PARTS * YB)

    def row_before(x):
        return pltpu.roll(x, 1, 0)

    def row_after(x):
        return pltpu.roll(x, WY - 1, 0)

    def lane_before(x):
        return jnp.where(first_lane, 0.0, pltpu.roll(x, 1, 1))

    def lane_after(x):
        return jnp.where(last_lane, 0.0, pltpu.roll(x, CZ - 1, 1))

    def coarse(index):
        if index < 0:
            cells = jnp.where(even_slab, chip[index + 2], core[index + 2])
            return jnp.where(slab > 0, cells, 0.0)
        if index >= CX:
            cells = jnp.where(even_slab, core[index - CX], chip[index - CX])
            return jnp.where(slab < last, cells, 0.0)
        return own[index]

    def spread(cells):
        middle = 0.75 * cells
        rows = [middle + 0.25 * row_before(cells), middle + 0.25 * row_after(cells)]
        result = []
        for cells_y in rows:
            middle = 0.75 * cells_y
            result.append(
                [middle + 0.25 * lane_before(cells_y), middle + 0.25 * lane_after(cells_y)]
            )
        return result

    def in_grid(plane):
        if plane < 0:
            return slab > 0
        if plane >= FX:
            return slab < last
        return None

    grids = {}
    for plane in range(-3, FX + 3):
        index, odd = plane // 2, plane % 2
        near = index + (1 if odd else -1)
        for which in (index, near):
            if which not in grids:
                grids[which] = spread(coarse(which))
        for old in [k for k in grids if k < min(index, near) - 1]:
            del grids[old]
        there = in_grid(plane)
        ok = inside if there is None else inside & there
        for odd_y in range(2):
            for odd_z in range(2):
                cells = 0.75 * grids[index][odd_y][odd_z] + 0.25 * grids[near][odd_y][odd_z]
                cells = cells + dots[plane + 3, odd_y, odd_z]
                dens[plane + 3, odd_y, odd_z] = jnp.where(ok, cells, 0.0)

    copy.wait()
    spread_blocks([(0, 1, 2, -10, 0)], flat, total, info, chosen)
    for plane in range(2):
        for odd_y in range(2):
            for odd_z in range(2):
                cells = total[odd_z, plane + 1, pl.ds(24 + odd_y, WY, stride=2), :]
                dens[plane, odd_y, odd_z] = dens[plane, odd_y, odd_z] + jnp.where(inside, cells, 0.0)

    def density(plane):
        return [[dens[plane + 3, odd_y, odd_z] for odd_z in range(2)] for odd_y in range(2)]

    def differences(field_y, field_z):
        along_y = [[None] * 2 for _ in range(2)]
        along_z = [[None] * 2 for _ in range(2)]
        for other in range(2):
            along_y[0][other] = field_y[1][other] - row_before(field_y[1][other])
            along_y[1][other] = row_after(field_y[0][other]) - field_y[0][other]
            along_z[other][0] = field_z[other][1] - lane_before(field_z[other][1])
            along_z[other][1] = lane_after(field_z[other][0]) - field_z[other][0]
        return along_y, along_z

    def store_flux(plane):
        there = in_grid(plane)
        ok = inside if there is None else inside & there
        here = density(plane)
        grad_y, grad_z = differences(here, here)
        flux_y = [[None] * 2 for _ in range(2)]
        flux_z = [[None] * 2 for _ in range(2)]
        by_density = [[None] * 2 for _ in range(2)]
        for odd_y in range(2):
            for odd_z in range(2):
                grad_x = dens[plane + 4, odd_y, odd_z] - dens[plane + 2, odd_y, odd_z]
                gy, gz = grad_y[odd_y][odd_z], grad_z[odd_y][odd_z]
                squared = grad_x * grad_x + gy * gy + gz * gz
                cells = jnp.where(ok, here[odd_y][odd_z], 1.0)
                inverse_root = jnp.exp(jnp.log(cells) * (-1.0 / 3.0))
                power_2 = inverse_root * inverse_root
                power_4 = power_2 * power_2
                inverse = 1.0 / (1.0 + DAMP * squared * (power_4 * power_4))
                by_density[odd_y][odd_z] = cells * power_2 * (B0 + inverse * (B1 + B2 * inverse))
                weight = jnp.where(ok, FLUX * power_4 * (inverse * inverse), 0.0)
                flux_x[plane + 2, odd_y, odd_z] = weight * grad_x
                flux_y[odd_y][odd_z] = weight * gy
                flux_z[odd_y][odd_z] = weight * gz
        if -1 <= plane <= FX:
            spread_y, spread_z = differences(flux_y, flux_z)
            for odd_y in range(2):
                for odd_z in range(2):
                    value[plane + 1, odd_y, odd_z] = by_density[odd_y][odd_z] - (
                        spread_y[odd_y][odd_z] + spread_z[odd_y][odd_z]
                    )

    for plane in range(-2, FX + 2):
        store_flux(plane)

    def potential(plane, odd_y, odd_z):
        there = in_grid(plane)
        ok = inside if there is None else inside & there
        cells = value[plane + 1, odd_y, odd_z] - (
            flux_x[plane + 3, odd_y, odd_z] - flux_x[plane + 1, odd_y, odd_z]
        )
        return jnp.where(ok, cells, 0.0)

    for index in range(CX):
        depth = [None, None]
        for odd_z in range(2):
            rows = []
            for odd_y in range(2):
                low = potential(2 * index - 1, odd_y, odd_z) + potential(2 * index + 2, odd_y, odd_z)
                mid = potential(2 * index, odd_y, odd_z) + potential(2 * index + 1, odd_y, odd_z)
                rows.append(0.125 * low + 0.375 * mid)
            depth[odd_z] = 0.125 * (row_before(rows[1]) + row_after(rows[0])) + 0.375 * (rows[0] + rows[1])
        cells = 0.125 * (lane_before(depth[1]) + lane_after(depth[0])) + 0.375 * (depth[0] + depth[1])
        for part_to in range(PARTS):
            out[part_to, YB * index : YB * index + YB] = cells[RIM : RIM + YB]


def join_kernel(pieces, out):
    for part in range(PARTS):
        for index in range(CX):
            out[index, YB * part : YB * part + YB] = pieces[part, YB * index : YB * index + YB]


SMEM = pl.BlockSpec(memory_space=pltpu.SMEM)
VMEM = pl.BlockSpec(memory_space=pltpu.VMEM)
F32 = jnp.float32


def is_dims(x):
    return isinstance(x, tuple) and all(isinstance(n, int) for n in x)


def call(kernel, name, out, in_specs, scratch=()):
    shapes = jax.tree.map(lambda dims: jax.ShapeDtypeStruct(dims, F32), out, is_leaf=is_dims)
    return pl.pallas_call(
        kernel,
        out_shape=shapes,
        in_specs=in_specs,
        out_specs=jax.tree.map(lambda dims: VMEM, out, is_leaf=is_dims),
        scratch_shapes=list(scratch),
        compiler_params=pltpu.CompilerParams(vmem_limit_bytes=32 * 2**20),
        name=name,
    )


def body(partial_density, moments, shape_functions, sphere_offsets, owned_count):
    slabs = lax.axis_size("dom")
    core_pairs = [(i, i ^ 1) for i in range(slabs)]
    second = [(i, (i + 2) % slabs) for i in range(slabs)]
    chip_pairs = []
    for b in range(PARTS):
        for i in range(slabs):
            j = i + 1 if i % 2 else i - 1
            there = (b, j) if 0 <= j < slabs else (b ^ 1, i)
            chip_pairs.append((b * slabs + i, there[0] * slabs + there[1]))

    windows = call(windows_kernel, "windows", (PARTS, CX, WY, CZ), [VMEM])(partial_density)
    windows = lax.all_to_all(windows, "band", 0, 0)

    packed, tail = call(
        blocks_kernel,
        "blocks",
        ((SLOTS, BLOCK + 128), (SLOTS, TAIL)),
        [VMEM] * 4,
    )(sphere_offsets, owned_count.reshape(1, 1), moments.T, shape_functions.transpose(1, 0, 2))
    dots_core = lax.ppermute(packed, "dom", core_pairs)
    dots_second = lax.ppermute(tail, "dom", second)
    dots_chip = lax.ppermute(packed, ("band", "dom"), chip_pairs)

    own, send_core, send_chip = call(
        own_kernel, "own_window", ((CX, WY, CZ), (2, WY, CZ), (4, WY, CZ)), [VMEM]
    )(windows)
    core = lax.ppermute(send_core, "dom", core_pairs)
    chip = lax.ppermute(send_chip, ("band", "dom"), chip_pairs)
    dots = call(
        place_kernel,
        "place_spheres",
        (FX + 6, 2, 2, WY, CZ),
        [VMEM] * 3,
        [
            pltpu.VMEM((64 + SLOTS * (2 * SBX + 3) * SBY + 128, 128), F32),
            pltpu.VMEM((2, 41, 80, CZ), F32),
            pltpu.VMEM((3, SLOTS, 128), jnp.int32),
            pltpu.SMEM((3, SLOTS, 128), jnp.int32),
            pltpu.SMEM((3 * SLOTS,), jnp.int32),
            pltpu.SemaphoreType.DMA,
        ],
    )(packed, dots_core, dots_chip)
    result = call(
        main_kernel,
        "potential_of",
        (PARTS, CX * YB, CZ),
        [VMEM] * 5,
        [
            pltpu.VMEM((FX + 6, 2, 2, WY, CZ), F32),
            pltpu.VMEM((FX + 4, 2, 2, WY, CZ), F32),
            pltpu.VMEM((FX + 2, 2, 2, WY, CZ), F32),
            pltpu.VMEM((64 + SLOTS * 2 * SBY + 128, 128), F32),
            pltpu.VMEM((2, 4, 80, CZ), F32),
            pltpu.VMEM((1, SLOTS, 128), jnp.int32),
            pltpu.SMEM((1, SLOTS, 128), jnp.int32),
            pltpu.SMEM((3 * SLOTS,), jnp.int32),
            pltpu.SemaphoreType.DMA,
        ],
    )(own, core, chip, dots, dots_second)
    gathered = lax.all_to_all(result, "band", 0, 0)
    return call(join_kernel, "join", (CX, PARTS * YB, CZ), [VMEM])(gathered)


def solution(mesh):
    return jax.shard_map(
        body,
        mesh=mesh,
        in_specs=(
            P("band", "dom", None, None),
            P(None, "dom"),
            P("dom", None, None),
            P(None, "dom"),
            P("dom"),
        ),
        out_specs=P("dom", None, None),
        check_vma=False,
    )
```

```python
import jax
import jax.numpy as jnp
from jax import lax
from jax.experimental import pallas as pl
from jax.experimental.pallas import tpu as pltpu
from jax.sharding import PartitionSpec as P

SLOTS = 8
SBX = 12
SBY = 24
SBZ = 24
BLOCK = SBX * SBY * SBZ
NL = 9
TAIL = 2 * SBY * SBZ + 128
CX = 6
FX = 12
RIM = 2
PARTS = 8
YB = 12
WY = 16
CZ = 128
FAR = -4096

KAPPA = 0.804
MU = 0.2195
PREFACTOR = -0.75 * (3.0 / 3.141592653589793) ** (1.0 / 3.0)
SCALE = 4.0 * (3.0 * 3.141592653589793**2) ** (2.0 / 3.0)
HALF_INVERSE = 0.5 / 0.2
DAMP = MU / KAPPA * HALF_INVERSE**2 / SCALE
B0 = PREFACTOR * 4.0 / 3.0 * (1.0 + KAPPA)
B1 = PREFACTOR * -4.0 * KAPPA
B2 = PREFACTOR * 8.0 / 3.0 * KAPPA
FLUX = 2.0 * HALF_INVERSE**2 * PREFACTOR * MU / SCALE


def windows_kernel(cells, windows):
    for part in range(PARTS):
        first = YB * part - RIM
        low, high = max(first, 0), min(first + WY, PARTS * YB)
        rows = cells[0, :, low:high, :]
        if low > first:
            rows = jnp.concatenate([jnp.zeros((CX, low - first, CZ), jnp.float32), rows], axis=1)
        if high < first + WY:
            rows = jnp.concatenate([rows, jnp.zeros((CX, first + WY - high, CZ), jnp.float32)], axis=1)
        windows[part] = rows


def blocks_kernel(offsets, count, moments, shapes, packed):
    row = lax.broadcasted_iota(jnp.int32, (SLOTS, SLOTS), 0)
    lane = lax.broadcasted_iota(jnp.int32, (SLOTS, SLOTS), 1)
    slot = lax.broadcasted_iota(jnp.int32, (SLOTS, 1), 0)
    alive = slot < count[...]
    where = lax.broadcasted_iota(jnp.int32, (SLOTS, 128), 1)
    info = jnp.zeros((SLOTS, 128), jnp.float32)
    for dim in range(3):
        values = jnp.broadcast_to(offsets[dim : dim + 1, :], (SLOTS, SLOTS)).astype(jnp.float32)
        column = jnp.sum(jnp.where(row == lane, values, 0.0), axis=1, keepdims=True)
        if dim == 1:
            column = jnp.where(alive, column, float(FAR))
        info = jnp.where(where == dim, column, info)
    packed[:, BLOCK : BLOCK + 128] = info
    weights = jnp.where(alive, moments[...].astype(jnp.float32), 0.0)
    step = BLOCK // 9
    for chunk in range(9):
        lanes = pl.ds(chunk * step, step)
        total = weights[:, 0:1] * shapes[0, :, lanes].astype(jnp.float32)
        for channel in range(1, NL):
            total = total + weights[:, channel : channel + 1] * shapes[channel, :, lanes].astype(
                jnp.float32
            )
        packed[:, lanes] = total


def line_up(read, depth_x, begin, flat):
    lane = lax.broadcasted_iota(jnp.int32, (SLOTS, 128), 1)
    tiles = {}
    for line in range(depth_x * SBY):
        tile, skip = divmod(line * SBZ, 128)
        for needed in (tile, tile + 1) if skip + SBZ > 128 else (tile,):
            if needed not in tiles:
                tiles = {k: v for k, v in tiles.items() if k >= tile}
                tiles[needed] = read(needed)
        cells = tiles[tile]
        if skip + SBZ > 128:
            cells = jnp.where(lane >= skip, cells, tiles[tile + 1])
        if skip:
            cells = pltpu.roll(cells, 128 - skip, 1)
        flat[pl.ds(64 + SLOTS * (begin * SBY + line), SLOTS), :] = jnp.where(lane < SBZ, cells, 0.0)


def whole_offsets(offsets, counts):
    lane = lax.broadcasted_iota(jnp.int32, (SLOTS, 128), 1)
    whole = offsets.astype(jnp.int32)
    row = jnp.max(jnp.where(lane == 0, whole, 0), axis=1, keepdims=True)
    there = whole - 2 * (YB * lax.axis_index("band") - RIM) + 24
    return jnp.where(lane == 1, jnp.where(counts(row), there, FAR), whole)


def spread_blocks(groups, flat, total, info, chosen):
    column = lax.broadcasted_iota(jnp.int32, (256, 256), 1)
    line = lax.rem(lax.broadcasted_iota(jnp.int32, (256, 256), 0), 128)
    inner_z = jnp.where(column < 128, 2 * column, 2 * column - 255) - line
    inner_z = jnp.where(line < SBZ, inner_z, -1)
    row_y = lax.broadcasted_iota(jnp.int32, (32, 128), 0)
    for first_source, sources, depth_x, first_plane, begin in groups:
        count = jnp.int32(0)
        for which in range(sources):
            for slot in range(SLOTS):
                col = info[first_source + which, slot, 1]
                chosen[count] = which * SLOTS + slot
                count = count + jnp.where((col > 0) & (col < 56), 1, 0)

        def one(index, carry):
            both = chosen[index]
            source = lax.shift_right_logical(both, 3)
            slot = both & (SLOTS - 1)
            row = info[first_source + source, slot, 0]
            col = info[first_source + source, slot, 1]
            depth = info[first_source + source, slot, 2]
            shift = lax.rem(col, 8)
            base = pl.multiple_of(col - shift, 8)
            held = (row_y >= shift) & (row_y < shift + SBY)
            origin = 64 + ((begin + SBX * source) * SBY - shift) * SLOTS + slot
            parts = []
            for x in range(depth_x):
                start = origin + x * SBY * SLOTS
                parts.append(jnp.where(held, flat[pl.ds(start, 32, stride=SLOTS), :], 0.0))
            block = jnp.concatenate(parts, axis=0)
            high = block.astype(jnp.bfloat16)
            low = (block - high.astype(jnp.float32)).astype(jnp.bfloat16)
            pick = jnp.where(inner_z == depth, 1.0, 0.0).astype(jnp.bfloat16)
            terms = jnp.concatenate([high, low], axis=1)
            spread = jnp.dot(terms, pick, preferred_element_type=jnp.float32)
            planes = pl.ds(row + first_plane - FX * source, depth_x)
            rows = pl.ds(base, 32)
            spread = spread.reshape(depth_x, 32, 256)
            for odd_z in range(2):
                half = spread[:, :, 128 * odd_z : 128 * odd_z + 128]
                total[odd_z, planes, rows, :] = total[odd_z, planes, rows, :] + half
            return carry

        lax.fori_loop(0, count, one, 0)


def place_kernel(own, core, chip, out, flat, total, whole, info, chosen, sem):
    slab = lax.axis_index("dom")
    even_slab = lax.rem(slab, 2) == 0
    last = lax.axis_size("dom") - 1
    lanes = pl.ds(BLOCK, 128)
    before = jnp.where(even_slab, chip[:, lanes], core[:, lanes])
    after = jnp.where(even_slab, core[:, lanes], chip[:, lanes])
    whole[0] = whole_offsets(own[:, lanes], lambda row: row >= 0)
    whole[1] = whole_offsets(before, lambda row: (row >= 0) & (slab > 0))
    whole[2] = whole_offsets(after, lambda row: (row < 3) & (slab < last))
    copy = pltpu.make_async_copy(whole, info, sem)
    copy.start()
    for odd_z in range(2):
        total[odd_z, pl.ds(11, 18), pl.ds(24, 32), :] = jnp.zeros((18, 32, 128), jnp.float32)

    def own_tile(tile):
        return own[:, 128 * tile : 128 * tile + 128]

    def before_tile(tile):
        lanes = pl.ds(128 * tile, 128)
        return jnp.where(even_slab, chip[:, lanes], core[:, lanes])

    def after_tile(tile):
        lanes = pl.ds(128 * tile, 128)
        return jnp.where(even_slab, core[:, lanes], chip[:, lanes])

    line_up(own_tile, SBX, 0, flat)
    line_up(before_tile, SBX, SBX, flat)
    line_up(after_tile, 3, 2 * SBX, flat)
    copy.wait()
    spread_blocks([(0, 2, SBX, 14, 0), (2, 1, 3, 26, 2 * SBX)], flat, total, info, chosen)
    for plane in range(FX + 6):
        for odd_y in range(2):
            for odd_z in range(2):
                rows = pl.ds(24 + odd_y, WY, stride=2)
                out[plane, odd_y, odd_z] = total[odd_z, plane + 11, rows, :]


def own_kernel(windows, other, own, send_chip):
    for plane in range(CX):
        cells = windows[0, plane]
        for part in range(1, PARTS):
            cells = cells + windows[part, plane]
        own[plane] = cells
    even_slab = lax.rem(lax.axis_index("dom"), 2) == 0
    send_chip[0:2] = jnp.where(even_slab, own[0:2], own[CX - 2 : CX])
    put_tail(other, send_chip)


def edge_kernel(own, other, send_core):
    even_slab = lax.rem(lax.axis_index("dom"), 2) == 0
    send_core[0:2] = jnp.where(even_slab, own[CX - 2 : CX], own[0:2])
    put_tail(other, send_core)


def put_tail(packed, out):
    for tile in range(TAIL // 128):
        first = BLOCK + 128 - TAIL + 128 * tile
        rows = pl.ds(SLOTS * (tile % 2), SLOTS)
        out[2 + tile // 2, rows] = packed[:, first : first + 128]


def main_kernel(own, core, chip, dots, out, dens, flux_x, value, flat, total, whole, info, chosen, sem):
    slab = lax.axis_index("dom")
    part = lax.axis_index("band")
    last = lax.axis_size("dom") - 1
    even_slab = lax.rem(slab, 2) == 0

    def second(tile):
        rows = pl.ds(SLOTS * (tile % 2), SLOTS)
        return jnp.where(even_slab, chip[2 + tile // 2, rows], core[2 + tile // 2, rows])

    whole[0] = whole_offsets(second(TAIL // 128 - 1), lambda row: (row >= 10) & (slab > 1))
    copy = pltpu.make_async_copy(whole, info, sem)
    copy.start()
    for odd_z in range(2):
        total[odd_z, pl.ds(0, 4), pl.ds(24, 32), :] = jnp.zeros((4, 32, CZ), jnp.float32)
    line_up(second, 2, 0, flat)
    lane = lax.broadcasted_iota(jnp.int32, (WY, CZ), 1)
    first_lane = lane == 0
    last_lane = lane == CZ - 1
    row = lax.broadcasted_iota(jnp.int32, (WY, CZ), 0) + (YB * part - RIM)
    inside = (row >= 0) & (row < PARTS * YB)

    def row_before(x):
        return pltpu.roll(x, 1, 0)

    def row_after(x):
        return pltpu.roll(x, WY - 1, 0)

    def lane_before(x):
        return jnp.where(first_lane, 0.0, pltpu.roll(x, 1, 1))

    def lane_after(x):
        return jnp.where(last_lane, 0.0, pltpu.roll(x, CZ - 1, 1))

    def coarse(index):
        if index < 0:
            cells = jnp.where(even_slab, chip[index + 2], core[index + 2])
            return jnp.where(slab > 0, cells, 0.0)
        if index >= CX:
            cells = jnp.where(even_slab, core[index - CX], chip[index - CX])
            return jnp.where(slab < last, cells, 0.0)
        return own[index]

    def spread(cells):
        middle = 0.75 * cells
        rows = [middle + 0.25 * row_before(cells), middle + 0.25 * row_after(cells)]
        result = []
        for cells_y in rows:
            middle = 0.75 * cells_y
            result.append(
                [middle + 0.25 * lane_before(cells_y), middle + 0.25 * lane_after(cells_y)]
            )
        return result

    def in_grid(plane):
        if plane < 0:
            return slab > 0
        if plane >= FX:
            return slab < last
        return None

    grids = {}
    for plane in range(-3, FX + 3):
        index, odd = plane // 2, plane % 2
        near = index + (1 if odd else -1)
        for which in (index, near):
            if which not in grids:
                grids[which] = spread(coarse(which))
        for old in [k for k in grids if k < min(index, near) - 1]:
            del grids[old]
        there = in_grid(plane)
        ok = inside if there is None else inside & there
        for odd_y in range(2):
            for odd_z in range(2):
                cells = 0.75 * grids[index][odd_y][odd_z] + 0.25 * grids[near][odd_y][odd_z]
                cells = cells + dots[plane + 3, odd_y, odd_z]
                dens[plane + 3, odd_y, odd_z] = jnp.where(ok, cells, 0.0)

    copy.wait()
    spread_blocks([(0, 1, 2, -10, 0)], flat, total, info, chosen)
    for plane in range(2):
        for odd_y in range(2):
            for odd_z in range(2):
                cells = total[odd_z, plane + 1, pl.ds(24 + odd_y, WY, stride=2), :]
                dens[plane, odd_y, odd_z] = dens[plane, odd_y, odd_z] + jnp.where(inside, cells, 0.0)

    def density(plane):
        return [[dens[plane + 3, odd_y, odd_z] for odd_z in range(2)] for odd_y in range(2)]

    def differences(field_y, field_z):
        along_y = [[None] * 2 for _ in range(2)]
        along_z = [[None] * 2 for _ in range(2)]
        for other in range(2):
            along_y[0][other] = field_y[1][other] - row_before(field_y[1][other])
            along_y[1][other] = row_after(field_y[0][other]) - field_y[0][other]
            along_z[other][0] = field_z[other][1] - lane_before(field_z[other][1])
            along_z[other][1] = lane_after(field_z[other][0]) - field_z[other][0]
        return along_y, along_z

    def store_flux(plane):
        there = in_grid(plane)
        ok = inside if there is None else inside & there
        here = density(plane)
        grad_y, grad_z = differences(here, here)
        flux_y = [[None] * 2 for _ in range(2)]
        flux_z = [[None] * 2 for _ in range(2)]
        by_density = [[None] * 2 for _ in range(2)]
        for odd_y in range(2):
            for odd_z in range(2):
                grad_x = dens[plane + 4, odd_y, odd_z] - dens[plane + 2, odd_y, odd_z]
                gy, gz = grad_y[odd_y][odd_z], grad_z[odd_y][odd_z]
                squared = grad_x * grad_x + gy * gy + gz * gz
                cells = jnp.where(ok, here[odd_y][odd_z], 1.0)
                inverse_root = jnp.exp(jnp.log(cells) * (-1.0 / 3.0))
                power_2 = inverse_root * inverse_root
                power_4 = power_2 * power_2
                inverse = 1.0 / (1.0 + DAMP * squared * (power_4 * power_4))
                by_density[odd_y][odd_z] = cells * power_2 * (B0 + inverse * (B1 + B2 * inverse))
                weight = jnp.where(ok, FLUX * power_4 * (inverse * inverse), 0.0)
                flux_x[plane + 2, odd_y, odd_z] = weight * grad_x
                flux_y[odd_y][odd_z] = weight * gy
                flux_z[odd_y][odd_z] = weight * gz
        if -1 <= plane <= FX:
            spread_y, spread_z = differences(flux_y, flux_z)
            for odd_y in range(2):
                for odd_z in range(2):
                    value[plane + 1, odd_y, odd_z] = by_density[odd_y][odd_z] - (
                        spread_y[odd_y][odd_z] + spread_z[odd_y][odd_z]
                    )

    for plane in range(-2, FX + 2):
        store_flux(plane)

    def potential(plane, odd_y, odd_z):
        there = in_grid(plane)
        ok = inside if there is None else inside & there
        cells = value[plane + 1, odd_y, odd_z] - (
            flux_x[plane + 3, odd_y, odd_z] - flux_x[plane + 1, odd_y, odd_z]
        )
        return jnp.where(ok, cells, 0.0)

    for index in range(CX):
        depth = [None, None]
        for odd_z in range(2):
            rows = []
            for odd_y in range(2):
                low = potential(2 * index - 1, odd_y, odd_z) + potential(2 * index + 2, odd_y, odd_z)
                mid = potential(2 * index, odd_y, odd_z) + potential(2 * index + 1, odd_y, odd_z)
                rows.append(0.125 * low + 0.375 * mid)
            depth[odd_z] = 0.125 * (row_before(rows[1]) + row_after(rows[0])) + 0.375 * (rows[0] + rows[1])
        cells = 0.125 * (lane_before(depth[1]) + lane_after(depth[0])) + 0.375 * (depth[0] + depth[1])
        for part_to in range(PARTS):
            out[part_to, YB * index : YB * index + YB] = cells[RIM : RIM + YB]


def join_kernel(pieces, out):
    for part in range(PARTS):
        for index in range(CX):
            out[index, YB * part : YB * part + YB] = pieces[part, YB * index : YB * index + YB]


SMEM = pl.BlockSpec(memory_space=pltpu.SMEM)
VMEM = pl.BlockSpec(memory_space=pltpu.VMEM)
F32 = jnp.float32


def is_dims(x):
    return isinstance(x, tuple) and all(isinstance(n, int) for n in x)


def call(kernel, name, out, in_specs, scratch=()):
    shapes = jax.tree.map(lambda dims: jax.ShapeDtypeStruct(dims, F32), out, is_leaf=is_dims)
    return pl.pallas_call(
        kernel,
        out_shape=shapes,
        in_specs=in_specs,
        out_specs=jax.tree.map(lambda dims: VMEM, out, is_leaf=is_dims),
        scratch_shapes=list(scratch),
        compiler_params=pltpu.CompilerParams(vmem_limit_bytes=32 * 2**20),
        name=name,
    )


def body(partial_density, moments, shape_functions, sphere_offsets, owned_count):
    slabs = lax.axis_size("dom")
    core_pairs = [(i, i ^ 1) for i in range(slabs)]
    chip_pairs = []
    for b in range(PARTS):
        for i in range(slabs):
            j = i + 1 if i % 2 else i - 1
            there = (b, j) if 0 <= j < slabs else (b ^ 1, i)
            chip_pairs.append((b * slabs + i, there[0] * slabs + there[1]))

    windows = call(windows_kernel, "windows", (PARTS, CX, WY, CZ), [VMEM])(partial_density)
    windows = lax.all_to_all(windows, "band", 0, 0)

    packed = call(
        blocks_kernel,
        "blocks",
        (SLOTS, BLOCK + 128),
        [VMEM] * 4,
    )(sphere_offsets, owned_count.reshape(1, 1), moments.T, shape_functions.transpose(1, 0, 2))
    dots_core = lax.ppermute(packed, "dom", core_pairs)
    dots_chip = lax.ppermute(packed, ("band", "dom"), chip_pairs)

    rim = (2 + TAIL // 256, WY, CZ)
    own, send_chip = call(own_kernel, "own_window", ((CX, WY, CZ), rim), [VMEM] * 2)(
        windows, dots_core
    )
    chip = lax.ppermute(send_chip, ("band", "dom"), chip_pairs)
    send_core = call(edge_kernel, "edge", rim, [VMEM] * 2)(own, dots_chip)
    core = lax.ppermute(send_core, "dom", core_pairs)
    dots = call(
        place_kernel,
        "place_spheres",
        (FX + 6, 2, 2, WY, CZ),
        [VMEM] * 3,
        [
            pltpu.VMEM((64 + SLOTS * (2 * SBX + 3) * SBY + 128, 128), F32),
            pltpu.VMEM((2, 41, 80, CZ), F32),
            pltpu.VMEM((3, SLOTS, 128), jnp.int32),
            pltpu.SMEM((3, SLOTS, 128), jnp.int32),
            pltpu.SMEM((3 * SLOTS,), jnp.int32),
            pltpu.SemaphoreType.DMA,
        ],
    )(packed, dots_core, dots_chip)
    result = call(
        main_kernel,
        "potential_of",
        (PARTS, CX * YB, CZ),
        [VMEM] * 4,
        [
            pltpu.VMEM((FX + 6, 2, 2, WY, CZ), F32),
            pltpu.VMEM((FX + 4, 2, 2, WY, CZ), F32),
            pltpu.VMEM((FX + 2, 2, 2, WY, CZ), F32),
            pltpu.VMEM((64 + SLOTS * 2 * SBY + 128, 128), F32),
            pltpu.VMEM((2, 4, 80, CZ), F32),
            pltpu.VMEM((1, SLOTS, 128), jnp.int32),
            pltpu.SMEM((1, SLOTS, 128), jnp.int32),
            pltpu.SMEM((3 * SLOTS,), jnp.int32),
            pltpu.SemaphoreType.DMA,
        ],
    )(own, core, chip, dots)
    gathered = lax.all_to_all(result, "band", 0, 0)
    return call(join_kernel, "join", (CX, PARTS * YB, CZ), [VMEM])(gathered)


def solution(mesh):
    return jax.shard_map(
        body,
        mesh=mesh,
        in_specs=(
            P("band", "dom", None, None),
            P(None, "dom"),
            P("dom", None, None),
            P(None, "dom"),
            P("dom"),
        ),
        out_specs=P("dom", None, None),
        check_vma=False,
    )
```

```python
import jax
import jax.numpy as jnp
from jax import lax
from jax.experimental import pallas as pl
from jax.experimental.pallas import tpu as pltpu
from jax.sharding import PartitionSpec as P

SLOTS = 8
SBX = 12
SBY = 24
SBZ = 24
BLOCK = SBX * SBY * SBZ
NL = 9
TAIL = 2 * SBY * SBZ + 128
CX = 6
FX = 12
RIM = 2
PARTS = 8
YB = 12
WY = 16
CZ = 128
FAR = -4096

KAPPA = 0.804
MU = 0.2195
PREFACTOR = -0.75 * (3.0 / 3.141592653589793) ** (1.0 / 3.0)
SCALE = 4.0 * (3.0 * 3.141592653589793**2) ** (2.0 / 3.0)
HALF_INVERSE = 0.5 / 0.2
DAMP = MU / KAPPA * HALF_INVERSE**2 / SCALE
B0 = PREFACTOR * 4.0 / 3.0 * (1.0 + KAPPA)
B1 = PREFACTOR * -4.0 * KAPPA
B2 = PREFACTOR * 8.0 / 3.0 * KAPPA
FLUX = 2.0 * HALF_INVERSE**2 * PREFACTOR * MU / SCALE


def windows_kernel(cells, windows):
    for part in range(PARTS):
        first = YB * part - RIM
        low, high = max(first, 0), min(first + WY, PARTS * YB)
        rows = cells[0, :, low:high, :]
        if low > first:
            rows = jnp.concatenate([jnp.zeros((CX, low - first, CZ), jnp.float32), rows], axis=1)
        if high < first + WY:
            rows = jnp.concatenate([rows, jnp.zeros((CX, first + WY - high, CZ), jnp.float32)], axis=1)
        windows[part] = rows


def blocks_kernel(offsets, count, moments, shapes, packed):
    row = lax.broadcasted_iota(jnp.int32, (SLOTS, SLOTS), 0)
    lane = lax.broadcasted_iota(jnp.int32, (SLOTS, SLOTS), 1)
    slot = lax.broadcasted_iota(jnp.int32, (SLOTS, 1), 0)
    alive = slot < count[...]
    where = lax.broadcasted_iota(jnp.int32, (SLOTS, 128), 1)
    info = jnp.zeros((SLOTS, 128), jnp.float32)
    for dim in range(3):
        values = jnp.broadcast_to(offsets[dim : dim + 1, :], (SLOTS, SLOTS)).astype(jnp.float32)
        column = jnp.sum(jnp.where(row == lane, values, 0.0), axis=1, keepdims=True)
        if dim == 1:
            column = jnp.where(alive, column, float(FAR))
        info = jnp.where(where == dim, column, info)
    packed[:, BLOCK : BLOCK + 128] = info
    weights = jnp.where(alive, moments[...].astype(jnp.float32), 0.0)
    step = BLOCK // 9
    for chunk in range(9):
        lanes = pl.ds(chunk * step, step)
        total = weights[:, 0:1] * shapes[0, :, lanes].astype(jnp.float32)
        for channel in range(1, NL):
            total = total + weights[:, channel : channel + 1] * shapes[channel, :, lanes].astype(
                jnp.float32
            )
        packed[:, lanes] = total


def line_up(read, depth_x, begin, flat):
    lane = lax.broadcasted_iota(jnp.int32, (SLOTS, 128), 1)
    tiles = {}
    for line in range(depth_x * SBY):
        tile, skip = divmod(line * SBZ, 128)
        for needed in (tile, tile + 1) if skip + SBZ > 128 else (tile,):
            if needed not in tiles:
                tiles = {k: v for k, v in tiles.items() if k >= tile}
                tiles[needed] = read(needed)
        cells = tiles[tile]
        if skip + SBZ > 128:
            cells = jnp.where(lane >= skip, cells, tiles[tile + 1])
        if skip:
            cells = pltpu.roll(cells, 128 - skip, 1)
        flat[pl.ds(64 + SLOTS * (begin * SBY + line), SLOTS), :] = jnp.where(lane < SBZ, cells, 0.0)


def whole_offsets(offsets, counts):
    lane = lax.broadcasted_iota(jnp.int32, (SLOTS, 128), 1)
    whole = offsets.astype(jnp.int32)
    row = jnp.max(jnp.where(lane == 0, whole, 0), axis=1, keepdims=True)
    there = whole - 2 * (YB * lax.axis_index("band") - RIM) + 24
    return jnp.where(lane == 1, jnp.where(counts(row), there, FAR), whole)


def spread_blocks(groups, flat, total, info, chosen):
    column = lax.broadcasted_iota(jnp.int32, (256, 256), 1)
    line = lax.rem(lax.broadcasted_iota(jnp.int32, (256, 256), 0), 128)
    inner_z = jnp.where(column < 128, 2 * column, 2 * column - 255) - line
    inner_z = jnp.where(line < SBZ, inner_z, -1)
    row_y = lax.broadcasted_iota(jnp.int32, (32, 128), 0)
    for first_source, sources, depth_x, first_plane, begin in groups:
        count = jnp.int32(0)
        for which in range(sources):
            for slot in range(SLOTS):
                col = info[first_source + which, slot, 1]
                chosen[count] = which * SLOTS + slot
                count = count + jnp.where((col > 0) & (col < 56), 1, 0)

        def one(index, carry):
            both = chosen[index]
            source = lax.shift_right_logical(both, 3)
            slot = both & (SLOTS - 1)
            row = info[first_source + source, slot, 0]
            col = info[first_source + source, slot, 1]
            depth = info[first_source + source, slot, 2]
            shift = lax.rem(col, 8)
            base = pl.multiple_of(col - shift, 8)
            held = (row_y >= shift) & (row_y < shift + SBY)
            origin = 64 + ((begin + SBX * source) * SBY - shift) * SLOTS + slot
            parts = []
            for x in range(depth_x):
                start = origin + x * SBY * SLOTS
                parts.append(jnp.where(held, flat[pl.ds(start, 32, stride=SLOTS), :], 0.0))
            block = jnp.concatenate(parts, axis=0)
            high = block.astype(jnp.bfloat16)
            low = (block - high.astype(jnp.float32)).astype(jnp.bfloat16)
            pick = jnp.where(inner_z == depth, 1.0, 0.0).astype(jnp.bfloat16)
            terms = jnp.concatenate([high, low], axis=1)
            spread = jnp.dot(terms, pick, preferred_element_type=jnp.float32)
            planes = pl.ds(row + first_plane - FX * source, depth_x)
            rows = pl.ds(base, 32)
            spread = spread.reshape(depth_x, 32, 256)
            for odd_z in range(2):
                half = spread[:, :, 128 * odd_z : 128 * odd_z + 128]
                total[odd_z, planes, rows, :] = total[odd_z, planes, rows, :] + half
            return carry

        lax.fori_loop(0, count, one, 0)


def place_kernel(own, core, chip, out, flat, total, whole, info, chosen, sem):
    slab = lax.axis_index("dom")
    even_slab = lax.rem(slab, 2) == 0
    last = lax.axis_size("dom") - 1
    lanes = pl.ds(BLOCK, 128)
    before = jnp.where(even_slab, chip[:, lanes], core[:, lanes])
    after = jnp.where(even_slab, core[:, lanes], chip[:, lanes])
    whole[0] = whole_offsets(own[:, lanes], lambda row: row >= 0)
    whole[1] = whole_offsets(before, lambda row: (row >= 0) & (slab > 0))
    whole[2] = whole_offsets(after, lambda row: (row < 3) & (slab < last))
    copy = pltpu.make_async_copy(whole, info, sem)
    copy.start()
    for odd_z in range(2):
        total[odd_z, pl.ds(11, 18), pl.ds(24, 32), :] = jnp.zeros((18, 32, 128), jnp.float32)

    def own_tile(tile):
        return own[:, 128 * tile : 128 * tile + 128]

    def before_tile(tile):
        lanes = pl.ds(128 * tile, 128)
        return jnp.where(even_slab, chip[:, lanes], core[:, lanes])

    def after_tile(tile):
        lanes = pl.ds(128 * tile, 128)
        return jnp.where(even_slab, core[:, lanes], chip[:, lanes])

    line_up(own_tile, SBX, 0, flat)
    line_up(before_tile, SBX, SBX, flat)
    line_up(after_tile, 3, 2 * SBX, flat)
    copy.wait()
    spread_blocks([(0, 2, SBX, 14, 0), (2, 1, 3, 26, 2 * SBX)], flat, total, info, chosen)
    for plane in range(FX + 6):
        for odd_y in range(2):
            for odd_z in range(2):
                rows = pl.ds(24 + odd_y, WY, stride=2)
                out[plane, odd_y, odd_z] = total[odd_z, plane + 11, rows, :]


def own_kernel(windows, other, own, send_chip):
    for plane in range(CX):
        cells = windows[0, plane]
        for part in range(1, PARTS):
            cells = cells + windows[part, plane]
        own[plane] = cells
    even_slab = lax.rem(lax.axis_index("dom"), 2) == 0
    send_chip[0:2] = jnp.where(even_slab, own[0:2], own[CX - 2 : CX])
    put_tail(other, send_chip)
    send_chip[2 + TAIL // 256 :] = own[0:4]


def edge_kernel(own, other, send_core):
    even_slab = lax.rem(lax.axis_index("dom"), 2) == 0
    send_core[0:2] = jnp.where(even_slab, own[CX - 2 : CX], own[0:2])
    put_tail(other, send_core)


def put_tail(packed, out):
    for tile in range(TAIL // 128):
        first = BLOCK + 128 - TAIL + 128 * tile
        rows = pl.ds(SLOTS * (tile % 2), SLOTS)
        out[2 + tile // 2, rows] = packed[:, first : first + 128]


def main_kernel(own, core, chip, dots, out, dens, flux_x, value, flat, total, whole, info, chosen, sem):
    slab = lax.axis_index("dom")
    part = lax.axis_index("band")
    last = lax.axis_size("dom") - 1
    even_slab = lax.rem(slab, 2) == 0

    def second(tile):
        rows = pl.ds(SLOTS * (tile % 2), SLOTS)
        return jnp.where(even_slab, chip[2 + tile // 2, rows], core[2 + tile // 2, rows])

    whole[0] = whole_offsets(second(TAIL // 128 - 1), lambda row: (row >= 10) & (slab > 1))
    copy = pltpu.make_async_copy(whole, info, sem)
    copy.start()
    for odd_z in range(2):
        total[odd_z, pl.ds(0, 4), pl.ds(24, 32), :] = jnp.zeros((4, 32, CZ), jnp.float32)
    line_up(second, 2, 0, flat)
    lane = lax.broadcasted_iota(jnp.int32, (WY, CZ), 1)
    first_lane = lane == 0
    last_lane = lane == CZ - 1
    row = lax.broadcasted_iota(jnp.int32, (WY, CZ), 0) + (YB * part - RIM)
    inside = (row >= 0) & (row < PARTS * YB)

    def row_before(x):
        return pltpu.roll(x, 1, 0)

    def row_after(x):
        return pltpu.roll(x, WY - 1, 0)

    def lane_before(x):
        return jnp.where(first_lane, 0.0, pltpu.roll(x, 1, 1))

    def lane_after(x):
        return jnp.where(last_lane, 0.0, pltpu.roll(x, CZ - 1, 1))

    def coarse(index):
        if index < 0:
            cells = jnp.where(even_slab, chip[index + 2], core[index + 2])
            return jnp.where(slab > 0, cells, 0.0)
        if index >= CX:
            cells = jnp.where(even_slab, core[index - CX], chip[index - CX])
            return jnp.where(slab < last, cells, 0.0)
        return own[index]

    def spread(cells):
        middle = 0.75 * cells
        rows = [middle + 0.25 * row_before(cells), middle + 0.25 * row_after(cells)]
        result = []
        for cells_y in rows:
            middle = 0.75 * cells_y
            result.append(
                [middle + 0.25 * lane_before(cells_y), middle + 0.25 * lane_after(cells_y)]
            )
        return result

    def in_grid(plane):
        if plane < 0:
            return slab > 0
        if plane >= FX:
            return slab < last
        return None

    grids = {}
    for plane in range(-3, FX + 3):
        index, odd = plane // 2, plane % 2
        near = index + (1 if odd else -1)
        for which in (index, near):
            if which not in grids:
                grids[which] = spread(coarse(which))
        for old in [k for k in grids if k < min(index, near) - 1]:
            del grids[old]
        there = in_grid(plane)
        ok = inside if there is None else inside & there
        for odd_y in range(2):
            for odd_z in range(2):
                cells = 0.75 * grids[index][odd_y][odd_z] + 0.25 * grids[near][odd_y][odd_z]
                cells = cells + dots[plane + 3, odd_y, odd_z]
                dens[plane + 3, odd_y, odd_z] = jnp.where(ok, cells, 0.0)

    copy.wait()
    spread_blocks([(0, 1, 2, -10, 0)], flat, total, info, chosen)
    for plane in range(2):
        for odd_y in range(2):
            for odd_z in range(2):
                cells = total[odd_z, plane + 1, pl.ds(24 + odd_y, WY, stride=2), :]
                dens[plane, odd_y, odd_z] = dens[plane, odd_y, odd_z] + jnp.where(inside, cells, 0.0)

    def density(plane):
        return [[dens[plane + 3, odd_y, odd_z] for odd_z in range(2)] for odd_y in range(2)]

    def differences(field_y, field_z):
        along_y = [[None] * 2 for _ in range(2)]
        along_z = [[None] * 2 for _ in range(2)]
        for other in range(2):
            along_y[0][other] = field_y[1][other] - row_before(field_y[1][other])
            along_y[1][other] = row_after(field_y[0][other]) - field_y[0][other]
            along_z[other][0] = field_z[other][1] - lane_before(field_z[other][1])
            along_z[other][1] = lane_after(field_z[other][0]) - field_z[other][0]
        return along_y, along_z

    def store_flux(plane):
        there = in_grid(plane)
        ok = inside if there is None else inside & there
        here = density(plane)
        grad_y, grad_z = differences(here, here)
        flux_y = [[None] * 2 for _ in range(2)]
        flux_z = [[None] * 2 for _ in range(2)]
        by_density = [[None] * 2 for _ in range(2)]
        for odd_y in range(2):
            for odd_z in range(2):
                grad_x = dens[plane + 4, odd_y, odd_z] - dens[plane + 2, odd_y, odd_z]
                gy, gz = grad_y[odd_y][odd_z], grad_z[odd_y][odd_z]
                squared = grad_x * grad_x + gy * gy + gz * gz
                cells = jnp.where(ok, here[odd_y][odd_z], 1.0)
                inverse_root = jnp.exp(jnp.log(cells) * (-1.0 / 3.0))
                power_2 = inverse_root * inverse_root
                power_4 = power_2 * power_2
                inverse = 1.0 / (1.0 + DAMP * squared * (power_4 * power_4))
                by_density[odd_y][odd_z] = cells * power_2 * (B0 + inverse * (B1 + B2 * inverse))
                weight = jnp.where(ok, FLUX * power_4 * (inverse * inverse), 0.0)
                flux_x[plane + 2, odd_y, odd_z] = weight * grad_x
                flux_y[odd_y][odd_z] = weight * gy
                flux_z[odd_y][odd_z] = weight * gz
        if -1 <= plane <= FX:
            spread_y, spread_z = differences(flux_y, flux_z)
            for odd_y in range(2):
                for odd_z in range(2):
                    value[plane + 1, odd_y, odd_z] = by_density[odd_y][odd_z] - (
                        spread_y[odd_y][odd_z] + spread_z[odd_y][odd_z]
                    )

    for plane in range(-2, FX + 2):
        store_flux(plane)

    def potential(plane, odd_y, odd_z):
        there = in_grid(plane)
        ok = inside if there is None else inside & there
        cells = value[plane + 1, odd_y, odd_z] - (
            flux_x[plane + 3, odd_y, odd_z] - flux_x[plane + 1, odd_y, odd_z]
        )
        return jnp.where(ok, cells, 0.0)

    for index in range(CX):
        depth = [None, None]
        for odd_z in range(2):
            rows = []
            for odd_y in range(2):
                low = potential(2 * index - 1, odd_y, odd_z) + potential(2 * index + 2, odd_y, odd_z)
                mid = potential(2 * index, odd_y, odd_z) + potential(2 * index + 1, odd_y, odd_z)
                rows.append(0.125 * low + 0.375 * mid)
            depth[odd_z] = 0.125 * (row_before(rows[1]) + row_after(rows[0])) + 0.375 * (rows[0] + rows[1])
        cells = 0.125 * (lane_before(depth[1]) + lane_after(depth[0])) + 0.375 * (depth[0] + depth[1])
        for part_to in range(PARTS):
            out[part_to, YB * index : YB * index + YB] = cells[RIM : RIM + YB]


def join_kernel(pieces, out):
    for part in range(PARTS):
        for index in range(CX):
            out[index, YB * part : YB * part + YB] = pieces[part, YB * index : YB * index + YB]


SMEM = pl.BlockSpec(memory_space=pltpu.SMEM)
VMEM = pl.BlockSpec(memory_space=pltpu.VMEM)
F32 = jnp.float32


def is_dims(x):
    return isinstance(x, tuple) and all(isinstance(n, int) for n in x)


def call(kernel, name, out, in_specs, scratch=()):
    shapes = jax.tree.map(lambda dims: jax.ShapeDtypeStruct(dims, F32), out, is_leaf=is_dims)
    return pl.pallas_call(
        kernel,
        out_shape=shapes,
        in_specs=in_specs,
        out_specs=jax.tree.map(lambda dims: VMEM, out, is_leaf=is_dims),
        scratch_shapes=list(scratch),
        compiler_params=pltpu.CompilerParams(vmem_limit_bytes=32 * 2**20),
        name=name,
    )


def body(partial_density, moments, shape_functions, sphere_offsets, owned_count):
    slabs = lax.axis_size("dom")
    core_pairs = [(i, i ^ 1) for i in range(slabs)]
    chip_pairs = []
    for b in range(PARTS):
        for i in range(slabs):
            j = i + 1 if i % 2 else i - 1
            there = (b, j) if 0 <= j < slabs else (b ^ 1, i)
            chip_pairs.append((b * slabs + i, there[0] * slabs + there[1]))

    windows = call(windows_kernel, "windows", (PARTS, CX, WY, CZ), [VMEM])(partial_density)
    windows = lax.all_to_all(windows, "band", 0, 0)

    packed = call(
        blocks_kernel,
        "blocks",
        (SLOTS, BLOCK + 128),
        [VMEM] * 4,
    )(sphere_offsets, owned_count.reshape(1, 1), moments.T, shape_functions.transpose(1, 0, 2))
    dots_core = lax.ppermute(packed, "dom", core_pairs)
    dots_chip = lax.ppermute(packed, ("band", "dom"), chip_pairs)

    rim = (2 + TAIL // 256, WY, CZ)
    own, send_chip = call(own_kernel, "own_window", ((CX, WY, CZ), (rim[0] + 4, WY, CZ)), [VMEM] * 2)(
        windows, dots_core
    )
    chip = lax.ppermute(send_chip, ("band", "dom"), chip_pairs)
    send_core = call(edge_kernel, "edge", rim, [VMEM] * 2)(own, dots_chip)
    core = lax.ppermute(send_core, "dom", core_pairs)
    dots = call(
        place_kernel,
        "place_spheres",
        (FX + 6, 2, 2, WY, CZ),
        [VMEM] * 3,
        [
            pltpu.VMEM((64 + SLOTS * (2 * SBX + 3) * SBY + 128, 128), F32),
            pltpu.VMEM((2, 41, 80, CZ), F32),
            pltpu.VMEM((3, SLOTS, 128), jnp.int32),
            pltpu.SMEM((3, SLOTS, 128), jnp.int32),
            pltpu.SMEM((3 * SLOTS,), jnp.int32),
            pltpu.SemaphoreType.DMA,
        ],
    )(packed, dots_core, dots_chip)
    result = call(
        main_kernel,
        "potential_of",
        (PARTS, CX * YB, CZ),
        [VMEM] * 4,
        [
            pltpu.VMEM((FX + 6, 2, 2, WY, CZ), F32),
            pltpu.VMEM((FX + 4, 2, 2, WY, CZ), F32),
            pltpu.VMEM((FX + 2, 2, 2, WY, CZ), F32),
            pltpu.VMEM((64 + SLOTS * 2 * SBY + 128, 128), F32),
            pltpu.VMEM((2, 4, 80, CZ), F32),
            pltpu.VMEM((1, SLOTS, 128), jnp.int32),
            pltpu.SMEM((1, SLOTS, 128), jnp.int32),
            pltpu.SMEM((3 * SLOTS,), jnp.int32),
            pltpu.SemaphoreType.DMA,
        ],
    )(own, core, chip, dots)
    gathered = lax.all_to_all(result, "band", 0, 0)
    return call(join_kernel, "join", (CX, PARTS * YB, CZ), [VMEM])(gathered)


def solution(mesh):
    return jax.shard_map(
        body,
        mesh=mesh,
        in_specs=(
            P("band", "dom", None, None),
            P(None, "dom"),
            P("dom", None, None),
            P(None, "dom"),
            P("dom"),
        ),
        out_specs=P("dom", None, None),
        check_vma=False,
    )
```
